256 devices in a mesh: tm: 32 (over y, z), gx: 4 (over x), gy: 2 (over core).
Axes of the slice: x: 4, y: 4, z: 8, core: 2. Of those that a mesh axis runs over, the one named last changes fastest.
Arguments:
- guesses: float32 [32, 64, 32, 256], P('tm', None, 'gx', 'gy'), may hold values from -6 to 6
- forcing: float32 [32, 64, 32, 256], P('tm', None, 'gx', 'gy'), may hold values from -4 to 4
- step_weight: float32 [16], replicated, may hold values from 0.25 to 1
- land_mask: int32 [32, 256], P('gx', 'gy'), may hold values 0 or 1
- fine_matrix: float32 [64, 64], replicated, may hold values from -1 to 1
- coupling: float32 [4, 64, 64], replicated, may hold values from -0.09375 to 0.09375
- coarse_matrix: float32 [64, 64], replicated, may hold values from -1 to 1
Outputs:
- updated_points: float32 [32, 64, 32, 256], P('tm', None, 'gx', 'gy')
- residual: float32 [32, 64, 32, 256], P('tm', None, 'gx', 'gy')
The draws below stay inside these ranges and needn't reach their ends.
All inputs are finite; a program needn't handle non-finite values. No bound on the sum of `land_mask` on one device may be relied on, other than what follows from the above.
Results may differ from the reference program's by a relative error of at most 0.0003.
Values sent between devices are 32-bit elements; how exact they have to be, the bound alone decides.
A program may use at most 64 MiB of HBM per device.

```python
import math
import jax
import jax.numpy as jnp
from jax import lax

DOF = 64
FACTOR = 16
NC = 32
NBX = 32
NBY = 256


def rotation_matrix(key, decay_rates):
    half_size = decay_rates.shape[0] // 2
    key_size, key_sign = jax.random.split(key)
    magnitude = jax.random.uniform(key_size, (half_size,), jnp.float32, 0.3, 1.0)
    orientation = jnp.where(jax.random.bernoulli(key_sign, 0.5, (half_size,)), 1.0, -1.0)
    angles = magnitude * orientation
    cosine = jnp.cos(angles)
    sine_part = jnp.sin(angles)
    upper_rates = decay_rates[:half_size]
    lower_rates = decay_rates[half_size:]
    upper = jnp.concatenate([jnp.diag(upper_rates * cosine), jnp.diag(-upper_rates * sine_part)], 1)
    lower = jnp.concatenate([jnp.diag(lower_rates * sine_part), jnp.diag(lower_rates * cosine)], 1)
    return jnp.concatenate([upper, lower], 0).astype(jnp.float32)


def draw_coarse_matrix(key, part):
    key_slow, key_fast, key_pick, key_turn = jax.random.split(jax.random.fold_in(key, 11), 4)
    slow_rates = jnp.exp(jnp.log(0.1) * jax.random.uniform(key_slow, (DOF,), jnp.float32, 0.3, 1.0) / NC)
    fast_rates = jax.random.uniform(key_fast, (DOF,), jnp.float32, 0.85, 0.92)
    keeps_state = jax.random.bernoulli(key_pick, 0.5, (DOF,))
    decay_rates = jnp.where(keeps_state, slow_rates, fast_rates)
    return rotation_matrix(key_turn, decay_rates)


def draw_fine_matrix(key, part):
    key_rate, key_turn = jax.random.split(jax.random.fold_in(key, 23))
    decay_rates = jnp.exp(jax.random.uniform(key_rate, (DOF,), jnp.float32, jnp.log(0.5), jnp.log(0.98)))
    return rotation_matrix(key_turn, decay_rates)


def place_ends(entries, own_key, low, high):
    longest = entries.shape.index(max(entries.shape))
    spots = []
    for shift in (0, 1):
        where = [jax.random.randint(jax.random.fold_in(own_key, axis), (), 0, length) for axis, length in enumerate(entries.shape)]
        where[longest] = (where[longest] + shift) % entries.shape[longest]
        spots.append(tuple(where))
    return entries.at[spots[0]].set(low).at[spots[1]].set(high)


def levels(own_key, extent, cuts, smallest, top_value):
    gain, own = 1.0, jax.random.fold_in(own_key, 6)
    for dim, shards_of in cuts:
        draws = jnp.exp(jax.random.uniform(jax.random.fold_in(own, dim), (shards_of,), jnp.float32, smallest / len(cuts), top_value / len(cuts)))
        gain = gain * jnp.repeat(draws, extent[dim] // shards_of).reshape([-1 if axis == dim else 1 for axis in range(len(extent))])
    return gain


def centred(key, extent, width, limit, cuts=(), kind=jnp.bfloat16):
    values = jax.random.normal(key, extent, jnp.float32) * width
    if len(cuts) > 0:
        values = levels(key, extent, cuts, -0.22, 0.18) * values
    return jnp.clip(values, min=-limit, max=limit).astype(kind)


def setup_inputs(seed: int = 0) -> dict:
    key_of = jax.random.split(jax.random.key(seed), 8)
    guesses = centred(key_of[0], (NC, DOF, NBX, NBY), 1.0, 6.0, ((0, 32), (2, 4), (3, 2)), jnp.float32)
    forcing = centred(key_of[1], (NC, DOF, NBX, NBY), 0.5, 4.0, ((0, 32), (2, 4), (3, 2)), jnp.float32)
    step_weight = jnp.clip(jnp.exp(jax.random.uniform(key_of[2], (FACTOR,), jnp.float32, math.log(0.25), math.log(1.0))), 0.25, 1.0)
    land_mask = place_ends((jax.random.randint(key_of[3], (NBX, NBY), 0, 4) < 3).astype(jnp.int32), jax.random.fold_in(key_of[3], 1), 0, 1)
    fine_matrix = draw_fine_matrix(jax.random.fold_in(key_of[7], 71), 0)
    coupling = centred(key_of[5], (4, DOF, DOF), (DOF * DOF) ** -0.5, 0.09375, (), jnp.float32)
    coarse_matrix = draw_coarse_matrix(jax.random.fold_in(key_of[7], 71), 0)
    return {"guesses": guesses, "forcing": forcing, "step_weight": step_weight, "land_mask": land_mask, "fine_matrix": fine_matrix, "coupling": coupling, "coarse_matrix": coarse_matrix}


def propagate(matrix, field):
    return jnp.einsum("ij,jxy->ixy", matrix, field, precision=lax.Precision.HIGHEST)


def fine_step(adjoint, source, fine_matrix, coupling, ocean_mask):
    padded = jnp.pad(adjoint, ((0, 0), (1, 1), (1, 1)))
    summed = propagate(fine_matrix, padded[:, 1:-1, 1:-1])
    summed = summed + propagate(coupling[0], padded[:, :-2, 1:-1])
    summed = summed + propagate(coupling[1], padded[:, 2:, 1:-1])
    summed = summed + propagate(coupling[2], padded[:, 1:-1, :-2])
    summed = summed + propagate(coupling[3], padded[:, 1:-1, 2:])
    return (summed + source) * ocean_mask


def reference(guesses, forcing, step_weight, land_mask, fine_matrix, coupling, coarse_matrix):
    ocean_mask = land_mask.astype(jnp.float32)[None]
    successors = jnp.concatenate([guesses[1:], jnp.zeros_like(guesses[:1])], 0)

    def relax(inputs):
        start_point, guess, source = inputs
        adjoint = start_point
        for step_index in range(FACTOR - 1, 0, -1):
            adjoint = fine_step(adjoint, step_weight[step_index] * source, fine_matrix, coupling, ocean_mask)
        final = fine_step(adjoint, step_weight[0] * source, fine_matrix, coupling, ocean_mask)
        return final - guess * ocean_mask

    residual = lax.map(relax, (successors, guesses, forcing))

    def backward(correction, residual_point):
        correction = propagate(coarse_matrix, correction) * ocean_mask + residual_point
        return correction, correction

    initial = jnp.zeros_like(guesses[0])
    unused, corrections = lax.scan(backward, initial, residual, reverse=True)
    return guesses + corrections, residual
```

```python
import functools

import jax
import jax.numpy as jnp
from jax import lax
from jax.experimental import pallas as pl
from jax.experimental.pallas import tpu as pltpu
from jax.sharding import PartitionSpec as P

MESH = pl.DeviceIdType.MESH
F32, BF16 = jnp.float32, jnp.bfloat16

NT, NZ, NY, NX = 32, 8, 4, 4
DOF, STEPS, LANES = 64, 16, 128
STRIP, HALO = 32, 16


def split(value):
    high = value.astype(BF16)
    return high, (value - high.astype(F32)).astype(BF16)


def right_operand(value):
    high, low = split(value)
    return jnp.concatenate([high, low, high, low], axis=0)


def left_operand(ref, rows, value, temporary):
    high = value.astype(BF16).astype(F32)
    low = value - high
    size = value.shape[0]
    for slot, part in enumerate((high, high, low, low)):
        temporary[0:size, 64 * slot : 64 * slot + 64] = part
    ref[rows, :] = temporary[0:size, :].astype(BF16)


def mul(left, right):
    return jnp.dot(left, right, preferred_element_type=F32)


def exact(left, right):
    return jnp.dot(left, right, precision=lax.Precision.HIGHEST, preferred_element_type=F32)


def kernel(
    g_hbm, f_hbm, weight, mask_hbm, fine, coupling, coarse,
    upd_hbm, res_hbm,
    gv, fv, g_edge, f_edge, mask_in, g_pack, f_pack, start, strip_f, strip_g, mask_s,
    fine_op, temporary, powers, power_op, state, product, last, dense, gathered, scan, total, totals,
    e_out, res_parts, e_parts, upd_v, res_v,
    load_sem, store_sem, edge_send, edge_recv, start_send, start_recv, f_send, f_recv, g_send, g_recv,
    d_send, d_recv, r_send, r_recv, t_send, t_recv, e_send, e_recv,
):
    tm, gx, gy = lax.axis_index("tm"), lax.axis_index("gx"), lax.axis_index("gy")
    y, z = tm // NZ, lax.rem(tm, NZ)
    owner = z // 2
    returns_here = owner == gx
    lane = lax.broadcasted_iota(jnp.int32, (64, LANES), 1)
    lane8 = lax.broadcasted_iota(jnp.int32, (8, LANES), 1)

    def remote(source, target, send, recv, device):
        return pltpu.make_async_remote_copy(
            src_ref=source, dst_ref=target, send_sem=send, recv_sem=recv, device_id=device, device_id_type=MESH
        )

    g_load = pltpu.make_async_copy(g_hbm, gv, load_sem.at[0])
    f_load = pltpu.make_async_copy(f_hbm, fv.at[pl.ds(0, 512)], load_sem.at[1])
    m_load = pltpu.make_async_copy(mask_hbm, mask_in, load_sem.at[2])
    g_load.start()
    m_load.start()
    f_load.start()

    barrier = pltpu.get_barrier_semaphore()

    def tell(device):
        pl.semaphore_signal(barrier, inc=1, device_id=device, device_id_type=MESH)

    later = lax.rem(tm + 1, NT)
    earlier = lax.rem(tm + NT - 1, NT)
    tell((tm, gx, 1 - gy))
    for q in range(NX):
        tell((later, q, gy))
    for d in range(1, NX):
        tell((tm, lax.rem(gx + d, NX), gy))
    for d in range(1, NZ):
        tell((y * NZ + lax.rem(z + d, NZ), gx, gy))
    for d in range(1, NY):
        tell((lax.rem(y + d, NY) * NZ + z, gx, gy))
    for h in range(2):
        for q in range(NX):
            @pl.when(jnp.logical_not(jnp.logical_and(2 * gx + h == z, gx == q)))
            def _():
                tell((y * NZ + 2 * gx + h, q, gy))

    m_load.wait()
    fv[512:520, :] = mask_in[...].astype(F32)
    g_load.wait()
    f_load.wait()

    def window(low_row, high_row, q):
        begin = STRIP * q - HALO
        where = lane[: low_row.shape[0]]
        return jnp.where(
            where < 64, pltpu.roll(low_row, (-begin) % LANES, 1), pltpu.roll(high_row, (64 - begin) % LANES, 1)
        )

    has_low = (gy == 1).astype(F32)
    has_high = (gy == 0).astype(F32)

    def extended(own, edge, q):
        where = lane[: own.shape[0]]
        if q == 0:
            return jnp.where(where >= LANES - HALO, edge * has_low, own)
        if q == NX - 1:
            return jnp.where(where < HALO, edge * has_high, own)
        return own

    def row(ref, x):
        return ref[pl.ds(x, DOF, stride=8), :]

    def pack(own, edge, out, q):
        for i in range(4):
            parts = []
            for x in (i, i + 4):
                mine = row(own, x)
                parts.append(extended(mine, row(edge, x), q) if q in (0, NX - 1) else mine)
            out[q, 64 * i : 64 * i + 64, :] = window(parts[0], parts[1], q)

    def pack_mask(q):
        mine = fv[512:520, :]
        if q in (0, NX - 1):
            mine = extended(mine, f_edge[512:520, :], q)
        f_pack[q, 256:264, :] = window(mine, pltpu.roll(mine, 4, 0), q)

    g_swap = remote(gv, g_edge, edge_send.at[0], edge_recv.at[0], (tm, gx, 1 - gy))
    f_swap = remote(fv, f_edge, edge_send.at[1], edge_recv.at[1], (tm, gx, 1 - gy))

    def start_copy(q):
        return remote(g_pack.at[q], start.at[gx], start_send.at[q], start_recv.at[gx], (earlier, q, gy))

    def strip_copy(source, target, send, recv, q):
        return remote(source.at[q], target.at[gx], send.at[q], recv.at[gx], (tm, q, gy))

    def strip_send(source, target, send, recv, q):
        @pl.when(gx != q)
        def _():
            strip_copy(source, target, send, recv, q).start()

        @pl.when(gx == q)
        def _():
            pltpu.make_async_copy(source.at[q], target.at[gx], recv.at[gx]).start()

    for q in (1, 2):
        pack(gv, None, g_pack, q)
    pl.semaphore_wait(barrier, 26 - returns_here.astype(jnp.int32))
    g_swap.start()
    f_swap.start()
    for q in (1, 2):
        start_copy(q).start()
    for q in (1, 2):
        pack(fv, None, f_pack, q)
        pack_mask(q)
        strip_send(f_pack, strip_f, f_send, f_recv, q)
    g_swap.wait_recv()
    for q in (0, 3):
        pack(gv, g_edge, g_pack, q)
        start_copy(q).start()
    f_swap.wait_recv()
    for q in (0, 3):
        pack(fv, f_edge, f_pack, q)
        pack_mask(q)
        strip_send(f_pack, strip_f, f_send, f_recv, q)
    for q in range(NX):
        strip_send(g_pack, strip_g, g_send, g_recv, q)

    left_operand(fine_op, pl.ds(0, 64), fine[...], temporary)
    left_operand(fine_op, pl.ds(64, 256), coupling[...], temporary)
    c1 = coarse[...]
    powers[0:64, :] = c1
    c2 = exact(c1, c1)
    powers[64:128, :] = c2
    powers[128:256, :] = exact(powers[0:128, :], c2)
    powers[256:512, :] = exact(powers[0:256, :], powers[192:256, :])
    c8 = powers[448:512, :]
    c16 = exact(c8, c8)
    left_operand(power_op, pl.ds(0, 512), powers[...], temporary)
    left_operand(power_op, pl.ds(512, 64), c16, temporary)

    is_last_interval = tm == NT - 1
    for q in range(NX):
        remote(g_pack.at[q], start.at[q], start_send.at[q], start_recv.at[q], (earlier, q, gy)).wait_recv()
        for i in range(4):
            begin = jnp.where(is_last_interval, 0.0, start[q, 64 * i : 64 * i + 64, :])
            high, low = split(begin)
            pair, half = 2 * q + i // 2, LANES * (i % 2)
            state[pair, 0:64, half : half + LANES] = high
            state[pair, 64:128, half : half + LANES] = low
    for q in range(NX):
        remote(f_pack.at[q], strip_f.at[q], f_send.at[q], f_recv.at[q], (tm, q, gy)).wait_recv()
        for i in range(4):
            mask_s[4 * q + i] = jnp.broadcast_to(strip_f[q, 256 + i : 257 + i, :], (8, LANES))

    def part(q, i, kind):
        half = LANES * (i % 2)
        return product[2 * q + i // 2, 64 * kind : 64 * kind + 64, half : half + LANES]

    def fine_step(k, final):
        for pair in range(8):
            rows = state[pair]
            product[pair] = mul(fine_op[...], jnp.concatenate([rows, rows], axis=0))
        scale = weight[k]
        low_half = lane < 64
        for q in range(NX):
            for i in range(4):
                if i > 0:
                    west = part(q, i - 1, 1)
                else:
                    before = part(q - 1, 3, 1) if q > 0 else jnp.zeros((64, LANES), F32)
                    west = pltpu.roll(jnp.where(low_half, part(q, 3, 1), before), 64, 1)
                if i < 3:
                    east = part(q, i + 1, 2)
                else:
                    after = part(q + 1, 0, 2) if q < NX - 1 else jnp.zeros((64, LANES), F32)
                    east = pltpu.roll(jnp.where(low_half, after, part(q, 0, 2)), 64, 1)
                south = pltpu.roll(part(q, i, 3), 1, 1)
                north = pltpu.roll(part(q, i, 4), LANES - 1, 1)
                value = (part(q, i, 0) + west) + (east + south) + (north + scale * strip_f[q, 64 * i : 64 * i + 64, :])
                mask = mask_s[4 * q + i]
                value = (value.reshape(8, 8, LANES) * mask[None]).reshape(64, LANES)
                if final:
                    last[4 * q + i] = value
                else:
                    high, low = split(value)
                    pair, half = 2 * q + i // 2, LANES * (i % 2)
                    state[pair, 0:64, half : half + LANES] = high
                    state[pair, 64:128, half : half + LANES] = low

    def body(step, carry):
        fine_step(STEPS - 1 - step, False)
        return carry

    lax.fori_loop(0, STEPS - 1, body, 0)
    fine_step(0, True)

    even_block = lax.rem(lane // STRIP, 2) == 0
    for q in range(NX):
        remote(g_pack.at[q], strip_g.at[q], g_send.at[q], g_recv.at[q], (tm, q, gy)).wait_recv()
        for h in range(2):
            pieces = []
            for i in (2 * h, 2 * h + 1):
                guess = strip_g[q, 64 * i : 64 * i + 64, :].reshape(8, 8, LANES) * mask_s[4 * q + i][None]
                pieces.append(last[4 * q + i] - guess.reshape(64, LANES))
            dense[2 * q + h] = jnp.where(
                even_block, pltpu.roll(pieces[0], LANES - HALO, 1), pltpu.roll(pieces[1], HALO, 1)
            )

    def dense_copy(k):
        return remote(dense.at[k], gathered.at[z], d_send.at[k], d_recv.at[z], (y * NZ + k, gx, gy))

    for k in range(NZ):
        @pl.when(z != k)
        def _():
            dense_copy(k).start()

        @pl.when(z == k)
        def _():
            pltpu.make_async_copy(dense.at[k], gathered.at[z], d_recv.at[z]).start()

    def residual_copy(q):
        return remote(dense.at[pl.ds(2 * q, 2)], res_parts.at[gx], r_send.at[q], r_recv.at[gx], (tm, q, gy))

    for q in range(NX):
        @pl.when(gx != q)
        def _():
            residual_copy(q).start()

        @pl.when(gx == q)
        def _():
            pltpu.make_async_copy(dense.at[pl.ds(2 * q, 2)], res_parts.at[gx], r_recv.at[gx]).start()

    for k in range(NZ):
        remote(dense.at[k], gathered.at[k], d_send.at[k], d_recv.at[k], (y * NZ + k, gx, gy)).wait_recv()
        scan[k] = gathered[k]
        if k > 0:
            terms = mul(power_op[0 : 64 * k, :], right_operand(gathered[k]))
            for p in range(1, k + 1):
                scan[k - p] += terms[64 * (p - 1) : 64 * p, :]
    total[...] = scan[0]

    def total_copy(d):
        return remote(total, totals.at[d - 1], t_send.at[d - 1], t_recv.at[d - 1], (lax.rem(y + NY - d, NY) * NZ + z, gx, gy))

    for d in range(1, NY):
        total_copy(d).start()

    def spread(parts, out, base):
        low_half = lane < 64
        for h in range(2):
            t = [parts[q, h] for q in range(NX)]
            a = [
                jnp.where(low_half, t[0], pltpu.roll(t[2], 64, 1)),
                jnp.where(low_half, t[1], pltpu.roll(t[3], 64, 1)),
                jnp.where(low_half, pltpu.roll(t[0], 64, 1), t[2]),
                jnp.where(low_half, pltpu.roll(t[1], 64, 1), t[3]),
            ]
            for m in range(2):
                first, second = a[2 * m], a[2 * m + 1]
                rows = (
                    jnp.where(even_block, first, pltpu.roll(second, STRIP, 1)),
                    jnp.where(even_block, pltpu.roll(first, LANES - STRIP, 1), second),
                )
                for n in range(2):
                    x = 2 * h + 4 * m + n
                    value = rows[n] if base is None else rows[n] + row(base, x)
                    out[pl.ds(x, DOF, stride=8), :] = value

    for q in range(NX):
        remote(dense.at[pl.ds(2 * q, 2)], res_parts.at[q], r_send.at[q], r_recv.at[q], (tm, q, gy)).wait_recv()
    spread(res_parts, res_v, None)
    res_store = pltpu.make_async_copy(res_v, res_hbm, store_sem.at[0])
    res_store.start()

    for d in range(1, NY):
        total_copy(d).wait_recv()
    zero = jnp.zeros((64, LANES), F32)
    groups = [jnp.where(y + d < NY, totals[d - 1], zero) for d in range(1, NY)]
    entering = groups[0] + mul(power_op[448:512, :], right_operand(groups[1])) + mul(
        power_op[512:576, :], right_operand(groups[2])
    )
    carried = mul(power_op[0:512, :], right_operand(entering))

    def e_copy(k):
        slot = 2 * gx + lax.rem(z, 2)
        return remote(e_out.at[k], e_parts.at[slot], e_send.at[k], e_recv.at[slot], (y * NZ + k, owner, gy))

    for k in range(NZ):
        e_out[k] = scan[k] + carried[64 * (NZ - 1 - k) : 64 * (NZ - k), :]
        here = jnp.logical_and(returns_here, z == k)

        @pl.when(jnp.logical_not(here))
        def _():
            e_copy(k).start()

        @pl.when(here)
        def _():
            slot = 2 * gx + lax.rem(z, 2)
            pltpu.make_async_copy(e_out.at[k], e_parts.at[slot], e_recv.at[slot]).start()

    for slot in range(8):
        remote(e_out.at[0], e_parts.at[slot], e_send.at[0], e_recv.at[slot], (y * NZ, owner, gy)).wait_recv()

    class Tiles:
        def __getitem__(self, index):
            return e_parts[2 * index[0] + index[1]]

    spread(Tiles(), upd_v, gv)
    upd_store = pltpu.make_async_copy(upd_v, upd_hbm, store_sem.at[1])
    upd_store.start()

    g_swap.wait_send()
    f_swap.wait_send()
    for q in range(NX):
        start_copy(q).wait_send()

        @pl.when(gx != q)
        def _():
            strip_copy(f_pack, strip_f, f_send, f_recv, q).wait_send()
            strip_copy(g_pack, strip_g, g_send, g_recv, q).wait_send()
            residual_copy(q).wait_send()

    for k in range(NZ):
        @pl.when(z != k)
        def _():
            dense_copy(k).wait_send()

        @pl.when(jnp.logical_not(jnp.logical_and(returns_here, z == k)))
        def _():
            e_copy(k).wait_send()

    for d in range(1, NY):
        total_copy(d).wait_send()
    res_store.wait()
    upd_store.wait()


def per_device(guesses, forcing, step_weight, land_mask, fine_matrix, coupling, coarse_matrix):
    vmem = pl.BlockSpec(memory_space=pltpu.VMEM)
    anywhere = pl.BlockSpec(memory_space=pl.ANY)
    flat = jax.ShapeDtypeStruct((DOF * 8, LANES), F32)
    dma = pltpu.SemaphoreType.DMA
    updated, residual = pl.pallas_call(
        kernel,
        out_shape=(flat, flat),
        in_specs=[anywhere, anywhere, pl.BlockSpec(memory_space=pltpu.SMEM), anywhere, vmem, vmem, vmem],
        out_specs=(anywhere, anywhere),
        scratch_shapes=[
            pltpu.VMEM((512, LANES), F32),
            pltpu.VMEM((520, LANES), F32),
            pltpu.VMEM((512, LANES), F32),
            pltpu.VMEM((520, LANES), F32),
            pltpu.VMEM((8, LANES), jnp.int32),
            pltpu.VMEM((NX, 256, LANES), F32),
            pltpu.VMEM((NX, 264, LANES), F32),
            pltpu.VMEM((NX, 256, LANES), F32),
            pltpu.VMEM((NX, 264, LANES), F32),
            pltpu.VMEM((NX, 256, LANES), F32),
            pltpu.VMEM((16, 8, LANES), F32),
            pltpu.VMEM((320, 256), BF16),
            pltpu.VMEM((512, 256), F32),
            pltpu.VMEM((512, DOF), F32),
            pltpu.VMEM((576, 256), BF16),
            pltpu.VMEM((8, 128, 256), BF16),
            pltpu.VMEM((8, 320, 256), F32),
            pltpu.VMEM((16, 64, LANES), F32),
            pltpu.VMEM((NZ, 64, LANES), F32),
            pltpu.VMEM((NZ, 64, LANES), F32),
            pltpu.VMEM((NZ, 64, LANES), F32),
            pltpu.VMEM((64, LANES), F32),
            pltpu.VMEM((NY - 1, 64, LANES), F32),
            pltpu.VMEM((NZ, 64, LANES), F32),
            pltpu.VMEM((NX, 2, 64, LANES), F32),
            pltpu.VMEM((8, 64, LANES), F32),
            pltpu.VMEM((512, LANES), F32),
            pltpu.VMEM((512, LANES), F32),
            dma((3,)), dma((2,)), dma((2,)), dma((2,)),
            dma((NX,)), dma((NX,)), dma((NX,)), dma((NX,)), dma((NX,)), dma((NX,)),
            dma((NZ,)), dma((NZ,)), dma((NX,)), dma((NX,)), dma((NY - 1,)), dma((NY - 1,)), dma((NZ,)), dma((8,)),
        ],
        compiler_params=pltpu.CompilerParams(
            collective_id=0, has_side_effects=True, vmem_limit_bytes=24 * 1024 * 1024
        ),
    )(
        guesses.reshape(DOF * 8, LANES), forcing.reshape(DOF * 8, LANES), step_weight, land_mask,
        fine_matrix, coupling.reshape(4 * DOF, DOF), coarse_matrix,
    )
    return updated.reshape(guesses.shape), residual.reshape(guesses.shape)


def solution(mesh):
    tiles = P("tm", None, "gx", "gy")
    return jax.shard_map(
        per_device,
        mesh=mesh,
        in_specs=(tiles, tiles, P(), P("gx", "gy"), P(), P(), P()),
        out_specs=(tiles, tiles),
        check_vma=False,
    )
```

```python
import functools

import jax
import jax.numpy as jnp
from jax import lax
from jax.experimental import pallas as pl
from jax.experimental.pallas import tpu as pltpu
from jax.sharding import PartitionSpec as P

MESH = pl.DeviceIdType.MESH
F32, BF16 = jnp.float32, jnp.bfloat16

NT, NZ, NY, NX = 32, 8, 4, 4
DOF, STEPS, LANES = 64, 16, 128
STRIP, HALO = 32, 16


def split(value):
    high = value.astype(BF16)
    return high, (value - high.astype(F32)).astype(BF16)


def right_operand(value):
    high, low = split(value)
    return jnp.concatenate([high, low, high, low], axis=0)


def left_operand(ref, rows, value, temporary):
    high = value.astype(BF16).astype(F32)
    low = value - high
    size = value.shape[0]
    for slot, part in enumerate((high, high, low, low)):
        temporary[0:size, 64 * slot : 64 * slot + 64] = part
    ref[rows, :] = temporary[0:size, :].astype(BF16)


def mul(left, right):
    return jnp.dot(left, right, preferred_element_type=F32)


def exact(left, right):
    return jnp.dot(left, right, precision=lax.Precision.HIGHEST, preferred_element_type=F32)


def kernel(
    g_hbm, f_hbm, weight, mask_hbm, fine_hbm, coupling_hbm, coarse_hbm,
    upd_v, res_v,
    gv, fv, g_edge, f_edge, mask_in, g_pack, f_pack, start, strip_f, strip_g, mask_s, g_dense,
    fine_op, temporary, powers, power_op, state, product, last, dense, packed, gathered, scan, sums,
    e_out, res_parts, e_parts,
    fine, coupling, coarse, load_sem, edge_send, edge_recv, start_send, start_recv, f_send, f_recv, g_send, g_recv,
    d_send, d_recv, r_send, r_recv, e_send, e_recv, group_sem,
):
    tm, gx, gy = lax.axis_index("tm"), lax.axis_index("gx"), lax.axis_index("gy")
    y, z = tm // NZ, lax.rem(tm, NZ)
    owner = z // 2
    returns_here = owner == gx
    lane = lax.broadcasted_iota(jnp.int32, (64, LANES), 1)
    lane8 = lax.broadcasted_iota(jnp.int32, (8, LANES), 1)

    def remote(source, target, send, recv, device):
        return pltpu.make_async_remote_copy(
            src_ref=source, dst_ref=target, send_sem=send, recv_sem=recv, device_id=device, device_id_type=MESH
        )

    g_load = pltpu.make_async_copy(g_hbm, gv, load_sem.at[0])
    f_load = pltpu.make_async_copy(f_hbm, fv.at[pl.ds(0, 512)], load_sem.at[1])
    m_load = pltpu.make_async_copy(mask_hbm, mask_in, load_sem.at[2])
    g_load.start()
    m_load.start()
    f_load.start()
    matrix_loads = [
        pltpu.make_async_copy(source, target, load_sem.at[3 + n])
        for n, (source, target) in enumerate(((fine_hbm, fine), (coupling_hbm, coupling), (coarse_hbm, coarse)))
    ]
    for load in matrix_loads:
        load.start()

    barrier = pltpu.get_barrier_semaphore()

    def tell(device):
        pl.semaphore_signal(barrier, inc=1, device_id=device, device_id_type=MESH)

    later = lax.rem(tm + 1, NT)
    earlier = lax.rem(tm + NT - 1, NT)
    tell((tm, gx, 1 - gy))
    for q in range(NX):
        tell((later, q, gy))
    for d in range(1, NX):
        tell((tm, lax.rem(gx + d, NX), gy))
    for d in range(1, NZ):
        tell((y * NZ + lax.rem(z + d, NZ), gx, gy))
    for d in range(1, NY):
        tell((lax.rem(y + d, NY) * NZ + z, gx, gy))

    m_load.wait()
    fv[512:520, :] = mask_in[...].astype(F32)
    g_load.wait()
    f_load.wait()

    def window(low_row, high_row, q):
        begin = STRIP * q - HALO
        where = lane[: low_row.shape[0]]
        return jnp.where(
            where < 64, pltpu.roll(low_row, (-begin) % LANES, 1), pltpu.roll(high_row, (64 - begin) % LANES, 1)
        )

    has_low = (gy == 1).astype(F32)
    has_high = (gy == 0).astype(F32)

    def extended(own, edge, q):
        where = lane[: own.shape[0]]
        if q == 0:
            return jnp.where(where >= LANES - HALO, edge * has_low, own)
        if q == NX - 1:
            return jnp.where(where < HALO, edge * has_high, own)
        return own

    def row(ref, x):
        return ref[pl.ds(x, DOF, stride=8), :]

    def pack(own, edge, out, q):
        for i in range(4):
            parts = []
            for x in (i, i + 4):
                mine = row(own, x)
                parts.append(extended(mine, row(edge, x), q) if q in (0, NX - 1) else mine)
            out[q, 64 * i : 64 * i + 64, :] = window(parts[0], parts[1], q)

    def pack_mask(q):
        mine = fv[512:520, :]
        if q in (0, NX - 1):
            mine = extended(mine, f_edge[512:520, :], q)
        f_pack[q, 256:264, :] = window(mine, pltpu.roll(mine, 4, 0), q)

    g_swap = remote(gv, g_edge, edge_send.at[0], edge_recv.at[0], (tm, gx, 1 - gy))
    f_swap = remote(fv, f_edge, edge_send.at[1], edge_recv.at[1], (tm, gx, 1 - gy))

    def start_copy(q):
        return remote(g_pack.at[q], start.at[gx], start_send.at[q], start_recv.at[gx], (earlier, q, gy))

    def strip_copy(source, target, send, recv, q):
        return remote(source.at[q], target.at[gx], send.at[q], recv.at[gx], (tm, q, gy))

    def strip_send(source, target, send, recv, q):
        @pl.when(gx != q)
        def _():
            strip_copy(source, target, send, recv, q).start()

        @pl.when(gx == q)
        def _():
            pltpu.make_async_copy(source.at[q], target.at[gx], recv.at[gx]).start()

    def columns_copy(p):
        return remote(packed.at[p], gathered.at[tm], d_send, d_recv, (p, gx, gy))

    def e_copy(p):
        slot = (lax.rem(z, 2) * 4 + y) * NX + gx
        return remote(e_out.at[p], e_parts.at[slot], e_send, e_recv, (p, owner, gy))

    def finish():
        g_swap.wait_send()
        f_swap.wait_send()
        for q in range(NX):
            start_copy(q).wait_send()

            @pl.when(gx != q)
            def _():
                strip_copy(f_pack, strip_f, f_send, f_recv, q).wait_send()
                strip_copy(g_dense, strip_g, g_send, g_recv, q).wait_send()
        for q in range(NX):
            @pl.when(gx != q)
            def _():
                strip_copy(dense, res_parts, r_send, r_recv, q).wait_send()
        some = pl.ds(0, NT - 1)
        pltpu.make_async_copy(packed.at[some], gathered.at[some], d_send).wait()
        @pl.when(returns_here)
        def _():
            some = pl.ds(0, NT - 1)
            pltpu.make_async_copy(e_out.at[some], e_parts.at[some], e_send).wait()

        @pl.when(jnp.logical_not(returns_here))
        def _():
            pltpu.make_async_copy(e_out, e_parts, e_send).wait()

    for q in (1, 2):
        pack(gv, None, g_pack, q)
    pl.semaphore_wait(barrier, 18)
    for d in range(1, NY):
        pl.semaphore_signal(group_sem, inc=1, device_id=(lax.rem(y + d, NY) * NZ + z, gx, gy), device_id_type=MESH)
    g_swap.start()
    f_swap.start()
    for q in (1, 2):
        start_copy(q).start()
    for q in (1, 2):
        pack(fv, None, f_pack, q)
        pack_mask(q)
        strip_send(f_pack, strip_f, f_send, f_recv, q)
    g_swap.wait_recv()
    for q in (0, 3):
        pack(gv, g_edge, g_pack, q)
        start_copy(q).start()
    f_swap.wait_recv()
    for q in (0, 3):
        pack(fv, f_edge, f_pack, q)
        pack_mask(q)
        strip_send(f_pack, strip_f, f_send, f_recv, q)

    even_block = lax.rem(lane8 // STRIP, 2) == 0
    low_half = lane8 < 64

    def exchange(t):
        a = (
            jnp.where(low_half, t[0], pltpu.roll(t[2], 64, 1)),
            jnp.where(low_half, t[1], pltpu.roll(t[3], 64, 1)),
            jnp.where(low_half, pltpu.roll(t[0], 64, 1), t[2]),
            jnp.where(low_half, pltpu.roll(t[1], 64, 1), t[3]),
        )
        out = []
        for first, second in ((a[0], a[1]), (a[2], a[3])):
            out.append(jnp.where(even_block, first, pltpu.roll(second, STRIP, 1)))
            out.append(jnp.where(even_block, pltpu.roll(first, LANES - STRIP, 1), second))
        return out

    def place(h, b):
        return 2 * h + 4 * (b // 2) + b % 2

    for h in range(2):
        for v in range(8):
            rows = [
                gv[pl.ds(64 * v + place(h, b), 8, stride=8), :] * fv[512 + place(h, b) : 513 + place(h, b), :]
                for b in range(4)
            ]
            for q, tile in enumerate(exchange(rows)):
                g_dense[q, h, 8 * v : 8 * v + 8, :] = tile

    for load in matrix_loads:
        load.wait()
    left_operand(fine_op, pl.ds(0, 64), fine[...], temporary)
    left_operand(fine_op, pl.ds(64, 256), coupling[...], temporary)
    c1 = coarse[...]
    powers[0:64, :] = c1
    c2 = exact(c1, c1)
    powers[64:128, :] = c2
    powers[128:256, :] = exact(powers[0:128, :], c2)
    powers[256:512, :] = exact(powers[0:256, :], powers[192:256, :])
    c8 = powers[448:512, :]
    c16 = exact(c8, c8)
    left_operand(power_op, pl.ds(0, 512), powers[...], temporary)
    left_operand(power_op, pl.ds(512, 64), c16, temporary)

    is_last_interval = tm == NT - 1
    for q in range(NX):
        remote(g_pack.at[q], start.at[q], start_send.at[q], start_recv.at[q], (earlier, q, gy)).wait_recv()
        for i in range(4):
            begin = jnp.where(is_last_interval, 0.0, start[q, 64 * i : 64 * i + 64, :])
            high, low = split(begin)
            pair, half = 2 * q + i // 2, LANES * (i % 2)
            state[pair, 0:64, half : half + LANES] = high
            state[pair, 64:128, half : half + LANES] = low
    for q in range(NX):
        remote(f_pack.at[q], strip_f.at[q], f_send.at[q], f_recv.at[q], (tm, q, gy)).wait_recv()
        for i in range(4):
            mask_s[4 * q + i] = jnp.broadcast_to(strip_f[q, 256 + i : 257 + i, :], (8, LANES))

    def part(q, i, kind):
        half = LANES * (i % 2)
        return product[2 * q + i // 2, 64 * kind : 64 * kind + 64, half : half + LANES]

    for q in range(NX):
        strip_send(g_dense, strip_g, g_send, g_recv, q)

    def fine_step(k, final):
        for pair in range(8):
            rows = state[pair]
            product[pair] = mul(fine_op[...], jnp.concatenate([rows, rows], axis=0))
        scale = weight[k]
        low_lanes = lane < 64
        for q in range(NX):
            for i in range(4):
                if i > 0:
                    west = part(q, i - 1, 1)
                else:
                    before = part(q - 1, 3, 1) if q > 0 else jnp.zeros((64, LANES), F32)
                    west = pltpu.roll(jnp.where(low_lanes, part(q, 3, 1), before), 64, 1)
                if i < 3:
                    east = part(q, i + 1, 2)
                else:
                    after = part(q + 1, 0, 2) if q < NX - 1 else jnp.zeros((64, LANES), F32)
                    east = pltpu.roll(jnp.where(low_lanes, after, part(q, 0, 2)), 64, 1)
                south = pltpu.roll(part(q, i, 3), 1, 1)
                north = pltpu.roll(part(q, i, 4), LANES - 1, 1)
                value = (part(q, i, 0) + west) + (east + south) + (north + scale * strip_f[q, 64 * i : 64 * i + 64, :])
                mask = mask_s[4 * q + i]
                value = (value.reshape(8, 8, LANES) * mask[None]).reshape(64, LANES)
                if final:
                    last[4 * q + i] = value
                else:
                    high, low = split(value)
                    pair, half = 2 * q + i // 2, LANES * (i % 2)
                    state[pair, 0:64, half : half + LANES] = high
                    state[pair, 64:128, half : half + LANES] = low

    def body(step, carry):
        fine_step(STEPS - 1 - step, False)
        return carry

    lax.fori_loop(0, STEPS - 1, body, 0)
    fine_step(0, True)

    even_lanes = lax.rem(lane // STRIP, 2) == 0
    for q in range(NX):
        remote(g_dense.at[q], strip_g.at[q], g_send.at[q], g_recv.at[q], (tm, q, gy)).wait_recv()
        for h in range(2):
            tile = jnp.where(
                even_lanes, pltpu.roll(last[4 * q + 2 * h], LANES - HALO, 1), pltpu.roll(last[4 * q + 2 * h + 1], HALO, 1)
            ) - strip_g[q, h]
            dense[q, h] = tile
            for u in range(2):
                pieces = exchange([tile[8 * (2 * c + u) : 8 * (2 * c + u) + 8] for c in range(4)])
                for b in range(4):
                    packed[b * NZ + 2 * q + h, 8 * u : 8 * u + 8, :] = pieces[b]

    pl.semaphore_wait(group_sem, NY - 1)
    pltpu.make_async_copy(packed.at[tm], gathered.at[tm], d_recv).start()

    def send_columns(i, carry):
        columns_copy(lax.rem(tm + i, NT)).start()
        return carry

    lax.fori_loop(1, NT, send_columns, 0)
    for q in range(NX):
        strip_send(dense, res_parts, r_send, r_recv, q)

    pltpu.make_async_copy(packed, gathered, d_recv).wait()
    for k in range(NZ):
        for u in range(2):
            pieces = exchange([gathered[i * NZ + k, 8 * u : 8 * u + 8, :] for i in range(NY)])
            for c in range(4):
                scan[k, 8 * (2 * c + u) : 8 * (2 * c + u) + 8, :] = pieces[c]
    for k in range(1, NZ):
        terms = mul(power_op[0 : 64 * k, :], right_operand(scan[k]))
        for p in range(1, k + 1):
            scan_sum = terms[64 * (p - 1) : 64 * p, :]
            if p == k:
                sums[0] = (sums[0] if k > 1 else scan[0]) + scan_sum
            else:
                sums[k - p] = (sums[k - p] if p > 1 else scan[k - p]) + scan_sum
    total = sums[0]
    zero = jnp.zeros((64, LANES), F32)

    def from_later(d):
        return jnp.where(lane < LANES - STRIP * d, pltpu.roll(total, LANES - STRIP * d, 1), zero)

    entering = from_later(1) + mul(power_op[448:512, :], right_operand(from_later(2))) + mul(
        power_op[512:576, :], right_operand(from_later(3))
    )
    carried = mul(power_op[0:512, :], right_operand(entering))
    for k in range(NZ):
        local = sums[k] if k < NZ - 1 else scan[k]
        tile = local + carried[64 * (NZ - 1 - k) : 64 * (NZ - k), :]
        for u in range(2):
            pieces = exchange([tile[8 * (2 * c + u) : 8 * (2 * c + u) + 8] for c in range(4)])
            for i in range(NY):
                e_out[i * NZ + k, 8 * u : 8 * u + 8, :] = pieces[i]

    @pl.when(returns_here)
    def _():
        slot = (lax.rem(z, 2) * 4 + y) * NX + gx
        pltpu.make_async_copy(e_out.at[tm], e_parts.at[slot], e_recv).start()

    @pl.when(jnp.logical_not(returns_here))
    def _():
        e_copy(tm).start()

    def send_result(i, carry):
        e_copy(lax.rem(tm + i, NT)).start()
        return carry

    lax.fori_loop(1, NT, send_result, 0)

    for q in range(NX):
        remote(dense.at[q], res_parts.at[q], r_send.at[q], r_recv.at[q], (tm, q, gy)).wait_recv()
    for h in range(2):
        for v in range(8):
            tiles = exchange([res_parts[q, h, 8 * v : 8 * v + 8, :] for q in range(NX)])
            for b in range(4):
                res_v[pl.ds(64 * v + place(h, b), 8, stride=8), :] = tiles[b]

    pltpu.make_async_copy(e_out, e_parts, e_recv).wait()
    for h in range(2):
        for b in range(4):
            for u in range(2):
                tiles = exchange([e_parts[(4 * h + b) * NX + q, 8 * u : 8 * u + 8, :] for q in range(NX)])
                for c in range(4):
                    where = pl.ds(64 * (2 * c + u) + place(h, b), 8, stride=8)
                    upd_v[where, :] = gv[where, :] + tiles[c]

    finish()


def per_device(guesses, forcing, step_weight, land_mask, fine_matrix, coupling, coarse_matrix):
    vmem = pl.BlockSpec(memory_space=pltpu.VMEM)
    hbm = pl.BlockSpec(memory_space=pltpu.HBM)
    flat = jax.ShapeDtypeStruct((DOF * 8, LANES), F32)
    dma = pltpu.SemaphoreType.DMA
    updated, residual = pl.pallas_call(
        kernel,
        out_shape=(flat, flat),
        in_specs=[hbm, hbm, pl.BlockSpec(memory_space=pltpu.SMEM), hbm, hbm, hbm, hbm],
        out_specs=(vmem, vmem),
        scratch_shapes=[
            pltpu.VMEM((512, LANES), F32),
            pltpu.VMEM((520, LANES), F32),
            pltpu.VMEM((512, LANES), F32),
            pltpu.VMEM((520, LANES), F32),
            pltpu.VMEM((8, LANES), jnp.int32),
            pltpu.VMEM((NX, 256, LANES), F32),
            pltpu.VMEM((NX, 264, LANES), F32),
            pltpu.VMEM((NX, 256, LANES), F32),
            pltpu.VMEM((NX, 264, LANES), F32),
            pltpu.VMEM((NX, 2, 64, LANES), F32),
            pltpu.VMEM((16, 8, LANES), F32),
            pltpu.VMEM((NX, 2, 64, LANES), F32),
            pltpu.VMEM((320, 256), BF16),
            pltpu.VMEM((512, 256), F32),
            pltpu.VMEM((512, DOF), F32),
            pltpu.VMEM((576, 256), BF16),
            pltpu.VMEM((8, 128, 256), BF16),
            pltpu.VMEM((8, 320, 256), F32),
            pltpu.VMEM((16, 64, LANES), F32),
            pltpu.VMEM((NX, 2, 64, LANES), F32),
            pltpu.VMEM((NT, 16, LANES), F32),
            pltpu.VMEM((NT, 16, LANES), F32),
            pltpu.VMEM((NZ, 64, LANES), F32),
            pltpu.VMEM((NZ - 1, 64, LANES), F32),
            pltpu.VMEM((NT, 16, LANES), F32),
            pltpu.VMEM((NX, 2, 64, LANES), F32),
            pltpu.VMEM((NT, 16, LANES), F32),
            pltpu.VMEM((DOF, DOF), F32),
            pltpu.VMEM((4 * DOF, DOF), F32),
            pltpu.VMEM((DOF, DOF), F32),
            dma((6,)), dma((2,)), dma((2,)),
            dma((NX,)), dma((NX,)), dma((NX,)), dma((NX,)), dma((NX,)), dma((NX,)),
            dma, dma, dma((NX,)), dma((NX,)), dma, dma, pltpu.SemaphoreType.REGULAR,
        ],
        compiler_params=pltpu.CompilerParams(
            collective_id=0, has_side_effects=True, vmem_limit_bytes=60 * 1024 * 1024
        ),
    )(
        guesses.reshape(DOF * 8, LANES), forcing.reshape(DOF * 8, LANES), step_weight, land_mask,
        fine_matrix, coupling.reshape(4 * DOF, DOF), coarse_matrix,
    )
    return updated.reshape(guesses.shape), residual.reshape(guesses.shape)


def solution(mesh):
    tiles = P("tm", None, "gx", "gy")
    return jax.shard_map(
        per_device,
        mesh=mesh,
        in_specs=(tiles, tiles, P(), P("gx", "gy"), P(), P(), P()),
        out_specs=(tiles, tiles),
        check_vma=False,
    )
```

```python
import functools

import jax
import jax.numpy as jnp
from jax import lax
from jax.experimental import pallas as pl
from jax.experimental.pallas import tpu as pltpu
from jax.sharding import PartitionSpec as P

MESH = pl.DeviceIdType.MESH
F32, BF16 = jnp.float32, jnp.bfloat16

NT, NZ, NY, NX = 32, 8, 4, 4
DOF, STEPS, LANES = 64, 16, 128
STRIP, HALO = 32, 16


def split(value):
    high = value.astype(BF16)
    return high, (value - high.astype(F32)).astype(BF16)


def right_operand(value):
    high, low = split(value)
    return jnp.concatenate([high, low, high, low], axis=0)


def left_operand(ref, rows, value, temporary):
    high = value.astype(BF16).astype(F32)
    low = value - high
    size = value.shape[0]
    for slot, part in enumerate((high, high, low, low)):
        temporary[0:size, 64 * slot : 64 * slot + 64] = part
    ref[rows, :] = temporary[0:size, :].astype(BF16)


def mul(left, right):
    return jnp.dot(left, right, preferred_element_type=F32)


def exact(left, right):
    return jnp.dot(left, right, precision=lax.Precision.HIGHEST, preferred_element_type=F32)


def kernel(
    g_hbm, f_hbm, weight, mask_hbm, fine_hbm, coupling_hbm, coarse_hbm,
    upd_v, res_v,
    gv, fv, g_edge, f_edge, mask_in, g_pack, f_pack, start, strip_f, strip_g, mask_s, g_dense,
    fine_op, temporary, powers, power_op, state, product, last, dense, packed, gathered, scan, sums,
    e_out, res_parts, e_parts,
    fine, coupling, coarse, load_sem, edge_send, edge_recv, start_send, start_recv, f_send, f_recv, g_send, g_recv,
    d_send, d_recv, r_send, r_recv, e_send, e_recv, group_sem,
):
    tm, gx, gy = lax.axis_index("tm"), lax.axis_index("gx"), lax.axis_index("gy")
    y, z = tm // NZ, lax.rem(tm, NZ)
    owner = lax.rem(z // 2 + NX - gx, NX)
    returns_here = owner == gx
    lane = lax.broadcasted_iota(jnp.int32, (64, LANES), 1)
    lane8 = lax.broadcasted_iota(jnp.int32, (8, LANES), 1)

    def remote(source, target, send, recv, device):
        return pltpu.make_async_remote_copy(
            src_ref=source, dst_ref=target, send_sem=send, recv_sem=recv, device_id=device, device_id_type=MESH
        )

    g_load = pltpu.make_async_copy(g_hbm, gv, load_sem.at[0])
    f_load = pltpu.make_async_copy(f_hbm, fv.at[pl.ds(0, 512)], load_sem.at[1])
    m_load = pltpu.make_async_copy(mask_hbm, mask_in, load_sem.at[2])
    g_load.start()
    m_load.start()
    f_load.start()
    matrix_loads = [
        pltpu.make_async_copy(source, target, load_sem.at[3 + n])
        for n, (source, target) in enumerate(((fine_hbm, fine), (coupling_hbm, coupling), (coarse_hbm, coarse)))
    ]
    for load in matrix_loads:
        load.start()

    barrier = pltpu.get_barrier_semaphore()

    def tell(device):
        pl.semaphore_signal(barrier, inc=1, device_id=device, device_id_type=MESH)

    later = lax.rem(tm + 1, NT)
    earlier = lax.rem(tm + NT - 1, NT)
    tell((tm, gx, 1 - gy))
    for q in range(NX):
        tell((later, q, gy))
    for d in range(1, NX):
        tell((tm, lax.rem(gx + d, NX), gy))
    for d in range(1, NZ):
        tell((y * NZ + lax.rem(z + d, NZ), gx, gy))
    for d in range(1, NY):
        tell((lax.rem(y + d, NY) * NZ + z, gx, gy))

    m_load.wait()
    fv[512:520, :] = mask_in[...].astype(F32)
    g_load.wait()
    f_load.wait()

    def window(low_row, high_row, q):
        begin = STRIP * q - HALO
        where = lane[: low_row.shape[0]]
        return jnp.where(
            where < 64, pltpu.roll(low_row, (-begin) % LANES, 1), pltpu.roll(high_row, (64 - begin) % LANES, 1)
        )

    has_low = (gy == 1).astype(F32)
    has_high = (gy == 0).astype(F32)

    def extended(own, edge, q):
        where = lane[: own.shape[0]]
        if q == 0:
            return jnp.where(where >= LANES - HALO, edge * has_low, own)
        if q == NX - 1:
            return jnp.where(where < HALO, edge * has_high, own)
        return own

    def row(ref, x):
        return ref[pl.ds(x, DOF, stride=8), :]

    def pack(own, edge, out, q):
        for i in range(4):
            parts = []
            for x in (i, i + 4):
                mine = row(own, x)
                parts.append(extended(mine, row(edge, x), q) if q in (0, NX - 1) else mine)
            out[q, 64 * i : 64 * i + 64, :] = window(parts[0], parts[1], q)

    def pack_mask(q):
        mine = fv[512:520, :]
        if q in (0, NX - 1):
            mine = extended(mine, f_edge[512:520, :], q)
        f_pack[q, 256:264, :] = window(mine, pltpu.roll(mine, 4, 0), q)

    g_swap = remote(gv, g_edge, edge_send.at[0], edge_recv.at[0], (tm, gx, 1 - gy))
    f_swap = remote(fv, f_edge, edge_send.at[1], edge_recv.at[1], (tm, gx, 1 - gy))

    def start_copy(q):
        return remote(g_pack.at[q], start.at[gx], start_send.at[q], start_recv.at[gx], (earlier, q, gy))

    def strip_copy(source, target, send, recv, q):
        return remote(source.at[q], target.at[gx], send.at[q], recv.at[gx], (tm, q, gy))

    def strip_send(source, target, send, recv, q):
        @pl.when(gx != q)
        def _():
            strip_copy(source, target, send, recv, q).start()

        @pl.when(gx == q)
        def _():
            pltpu.make_async_copy(source.at[q], target.at[gx], recv.at[gx]).start()

    def columns_copy(p):
        return remote(packed.at[p], gathered.at[tm], d_send, d_recv, (p, gx, gy))

    def e_copy(p):
        slot = (lax.rem(z, 2) * 4 + y) * NX + gx
        return remote(e_out.at[p], e_parts.at[slot], e_send, e_recv, (p, owner, gy))

    def finish():
        g_swap.wait_send()
        f_swap.wait_send()
        for q in range(NX):
            start_copy(q).wait_send()

            @pl.when(gx != q)
            def _():
                strip_copy(f_pack, strip_f, f_send, f_recv, q).wait_send()
                strip_copy(g_dense, strip_g, g_send, g_recv, q).wait_send()
        for q in range(NX):
            @pl.when(gx != q)
            def _():
                strip_copy(dense, res_parts, r_send, r_recv, q).wait_send()
        some = pl.ds(0, NT - 1)
        pltpu.make_async_copy(packed.at[some], gathered.at[some], d_send).wait()
        @pl.when(returns_here)
        def _():
            some = pl.ds(0, NT - 1)
            pltpu.make_async_copy(e_out.at[some], e_parts.at[some], e_send).wait()

        @pl.when(jnp.logical_not(returns_here))
        def _():
            pltpu.make_async_copy(e_out, e_parts, e_send).wait()

    for q in (1, 2):
        pack(gv, None, g_pack, q)
    pl.semaphore_wait(barrier, 18)
    for d in range(1, NY):
        pl.semaphore_signal(group_sem, inc=1, device_id=(lax.rem(y + d, NY) * NZ + z, gx, gy), device_id_type=MESH)
    g_swap.start()
    f_swap.start()
    qa = 1 + lax.rem(gx, 2)
    for q in (qa, 3 - qa):
        start_copy(q).start()
    g_swap.wait_recv()
    for q in (0, 3):
        pack(gv, g_edge, g_pack, q)
    qc = 3 * lax.rem(gx, 2)
    for q in (qc, 3 - qc):
        start_copy(q).start()
    for q in (1, 2):
        pack(fv, None, f_pack, q)
        pack_mask(q)
    f_swap.wait_recv()
    for q in (0, 3):
        pack(fv, f_edge, f_pack, q)
        pack_mask(q)
    for d in range(1, NX):
        strip_copy(f_pack, strip_f, f_send, f_recv, lax.rem(gx + d, NX)).start()
    pltpu.make_async_copy(f_pack.at[gx], strip_f.at[gx], f_recv.at[gx]).start()

    even_block = lax.rem(lane8 // STRIP, 2) == 0
    low_half = lane8 < 64

    def exchange(t):
        a = (
            jnp.where(low_half, t[0], pltpu.roll(t[2], 64, 1)),
            jnp.where(low_half, t[1], pltpu.roll(t[3], 64, 1)),
            jnp.where(low_half, pltpu.roll(t[0], 64, 1), t[2]),
            jnp.where(low_half, pltpu.roll(t[1], 64, 1), t[3]),
        )
        out = []
        for first, second in ((a[0], a[1]), (a[2], a[3])):
            out.append(jnp.where(even_block, first, pltpu.roll(second, STRIP, 1)))
            out.append(jnp.where(even_block, pltpu.roll(first, LANES - STRIP, 1), second))
        return out

    def place(h, b):
        return 2 * h + 4 * (b // 2) + b % 2

    for h in range(2):
        for v in range(8):
            rows = [
                gv[pl.ds(64 * v + place(h, b), 8, stride=8), :] * fv[512 + place(h, b) : 513 + place(h, b), :]
                for b in range(4)
            ]
            for q, tile in enumerate(exchange(rows)):
                g_dense[q, h, 8 * v : 8 * v + 8, :] = tile

    for load in matrix_loads:
        load.wait()
    left_operand(fine_op, pl.ds(0, 64), fine[...], temporary)
    left_operand(fine_op, pl.ds(64, 128), coupling[128:256, :], temporary)
    left_operand(fine_op, pl.ds(192, 128), coupling[0:128, :], temporary)
    c1 = coarse[...]
    powers[0:64, :] = c1
    c2 = exact(c1, c1)
    powers[64:128, :] = c2
    powers[128:256, :] = exact(powers[0:128, :], c2)
    powers[256:512, :] = exact(powers[0:256, :], powers[192:256, :])
    c8 = powers[448:512, :]
    c16 = exact(c8, c8)
    left_operand(power_op, pl.ds(0, 512), powers[...], temporary)
    left_operand(power_op, pl.ds(512, 64), c16, temporary)

    is_last_interval = tm == NT - 1
    for q in range(NX):
        remote(g_pack.at[q], start.at[q], start_send.at[q], start_recv.at[q], (earlier, q, gy)).wait_recv()
        for i in range(4):
            begin = jnp.where(is_last_interval, 0.0, start[q, 64 * i : 64 * i + 64, :])
            high, low = split(begin)
            pair, half = 2 * q + i // 2, LANES * (i % 2)
            state[pair, 0:64, half : half + LANES] = high
            state[pair, 64:128, half : half + LANES] = low
    for q in range(NX):
        remote(f_pack.at[q], strip_f.at[q], f_send.at[q], f_recv.at[q], (tm, q, gy)).wait_recv()
        for i in range(4):
            mask_s[4 * q + i] = jnp.broadcast_to(strip_f[q, 256 + i : 257 + i, :], (8, LANES))

    def part(q, i, kind):
        half = LANES * (i % 2)
        return product[2 * q + i // 2, 64 * kind : 64 * kind + 64, half : half + LANES]

    for d in range(1, NX):
        strip_copy(g_dense, strip_g, g_send, g_recv, lax.rem(gx + d, NX)).start()
    pltpu.make_async_copy(g_dense.at[gx], strip_g.at[gx], g_recv.at[gx]).start()

    def fine_step(k, final):
        for pair in range(8):
            rows = state[pair]
            terms = mul(fine_op[:, 0:192], jnp.concatenate([rows, rows[0:64]], axis=0))
            for half in (slice(0, LANES), slice(LANES, 2 * LANES)):
                south = pltpu.roll(terms[64:128, half], 1, 1)
                north = pltpu.roll(terms[128:192, half], LANES - 1, 1)
                product[pair, 0:64, half] = terms[0:64, half] + (south + north)
            product[pair, 64:192] = terms[192:320]
        scale = weight[k]
        low_lanes = lane < 64
        for q in range(NX):
            for i in range(4):
                if i > 0:
                    west = part(q, i - 1, 1)
                else:
                    before = part(q - 1, 3, 1) if q > 0 else jnp.zeros((64, LANES), F32)
                    west = pltpu.roll(jnp.where(low_lanes, part(q, 3, 1), before), 64, 1)
                if i < 3:
                    east = part(q, i + 1, 2)
                else:
                    after = part(q + 1, 0, 2) if q < NX - 1 else jnp.zeros((64, LANES), F32)
                    east = pltpu.roll(jnp.where(low_lanes, after, part(q, 0, 2)), 64, 1)
                value = (part(q, i, 0) + scale * strip_f[q, 64 * i : 64 * i + 64, :]) + (west + east)
                mask = mask_s[4 * q + i]
                value = (value.reshape(8, 8, LANES) * mask[None]).reshape(64, LANES)
                if final:
                    last[4 * q + i] = value
                else:
                    high, low = split(value)
                    pair, half = 2 * q + i // 2, LANES * (i % 2)
                    state[pair, 0:64, half : half + LANES] = high
                    state[pair, 64:128, half : half + LANES] = low

    def body(step, carry):
        fine_step(STEPS - 1 - step, False)
        return carry

    lax.fori_loop(0, STEPS - 1, body, 0)
    fine_step(0, True)

    even_lanes = lax.rem(lane // STRIP, 2) == 0
    for q in range(NX):
        remote(g_dense.at[q], strip_g.at[q], g_send.at[q], g_recv.at[q], (tm, q, gy)).wait_recv()
        for h in range(2):
            tile = jnp.where(
                even_lanes, pltpu.roll(last[4 * q + 2 * h], LANES - HALO, 1), pltpu.roll(last[4 * q + 2 * h + 1], HALO, 1)
            ) - strip_g[q, h]
            dense[q, h] = tile
            for u in range(2):
                pieces = exchange([tile[8 * (2 * c + u) : 8 * (2 * c + u) + 8] for c in range(4)])
                for b in range(4):
                    packed[b * NZ + 2 * lax.rem(q + gx, NX) + h, 8 * u : 8 * u + 8, :] = pieces[b]

    pl.semaphore_wait(group_sem, NY - 1)
    pltpu.make_async_copy(packed.at[tm], gathered.at[tm], d_recv).start()

    def send_columns(i, carry):
        columns_copy(lax.rem(tm + i, NT)).start()
        return carry

    lax.fori_loop(1, NT, send_columns, 0)
    for d in range(1, NX):
        strip_copy(dense, res_parts, r_send, r_recv, lax.rem(gx + d, NX)).start()
    pltpu.make_async_copy(dense.at[gx], res_parts.at[gx], r_recv.at[gx]).start()

    pltpu.make_async_copy(packed, gathered, d_recv).wait()
    for k in range(NZ):
        for u in range(2):
            pieces = exchange([gathered[i * NZ + k, 8 * u : 8 * u + 8, :] for i in range(NY)])
            for c in range(4):
                scan[k, 8 * (2 * c + u) : 8 * (2 * c + u) + 8, :] = pieces[c]
    for k in range(1, NZ):
        terms = mul(power_op[0 : 64 * k, :], right_operand(scan[k]))
        for p in range(1, k + 1):
            scan_sum = terms[64 * (p - 1) : 64 * p, :]
            if p == k:
                sums[0] = (sums[0] if k > 1 else scan[0]) + scan_sum
            else:
                sums[k - p] = (sums[k - p] if p > 1 else scan[k - p]) + scan_sum
    total = sums[0]
    zero = jnp.zeros((64, LANES), F32)

    def from_later(d):
        return jnp.where(lane < LANES - STRIP * d, pltpu.roll(total, LANES - STRIP * d, 1), zero)

    entering = from_later(1) + mul(power_op[448:512, :], right_operand(from_later(2))) + mul(
        power_op[512:576, :], right_operand(from_later(3))
    )
    carried = mul(power_op[0:512, :], right_operand(entering))
    for k in range(NZ):
        local = sums[k] if k < NZ - 1 else scan[k]
        tile = local + carried[64 * (NZ - 1 - k) : 64 * (NZ - k), :]
        for u in range(2):
            pieces = exchange([tile[8 * (2 * c + u) : 8 * (2 * c + u) + 8] for c in range(4)])
            for i in range(NY):
                e_out[i * NZ + k, 8 * u : 8 * u + 8, :] = pieces[i]

    @pl.when(returns_here)
    def _():
        slot = (lax.rem(z, 2) * 4 + y) * NX + gx
        pltpu.make_async_copy(e_out.at[tm], e_parts.at[slot], e_recv).start()

    @pl.when(jnp.logical_not(returns_here))
    def _():
        e_copy(tm).start()

    def send_result(i, carry):
        e_copy(lax.rem(tm + i, NT)).start()
        return carry

    lax.fori_loop(1, NT, send_result, 0)

    for q in range(NX):
        remote(dense.at[q], res_parts.at[q], r_send.at[q], r_recv.at[q], (tm, q, gy)).wait_recv()
    for h in range(2):
        for v in range(8):
            tiles = exchange([res_parts[q, h, 8 * v : 8 * v + 8, :] for q in range(NX)])
            for b in range(4):
                res_v[pl.ds(64 * v + place(h, b), 8, stride=8), :] = tiles[b]

    pltpu.make_async_copy(e_out, e_parts, e_recv).wait()
    for h in range(2):
        for b in range(4):
            for u in range(2):
                tiles = exchange([e_parts[(4 * h + b) * NX + q, 8 * u : 8 * u + 8, :] for q in range(NX)])
                for c in range(4):
                    where = pl.ds(64 * (2 * c + u) + place(h, b), 8, stride=8)
                    upd_v[where, :] = gv[where, :] + tiles[c]

    finish()


def per_device(guesses, forcing, step_weight, land_mask, fine_matrix, coupling, coarse_matrix):
    vmem = pl.BlockSpec(memory_space=pltpu.VMEM)
    hbm = pl.BlockSpec(memory_space=pltpu.HBM)

    def in_hbm(value):
        return pltpu.with_memory_space_constraint(value, pltpu.HBM)

    flat = jax.ShapeDtypeStruct((DOF * 8, LANES), F32)
    dma = pltpu.SemaphoreType.DMA
    updated, residual = pl.pallas_call(
        kernel,
        out_shape=(flat, flat),
        in_specs=[hbm, hbm, pl.BlockSpec(memory_space=pltpu.SMEM), hbm, hbm, hbm, hbm],
        out_specs=(vmem, vmem),
        scratch_shapes=[
            pltpu.VMEM((512, LANES), F32),
            pltpu.VMEM((520, LANES), F32),
            pltpu.VMEM((512, LANES), F32),
            pltpu.VMEM((520, LANES), F32),
            pltpu.VMEM((8, LANES), jnp.int32),
            pltpu.VMEM((NX, 256, LANES), F32),
            pltpu.VMEM((NX, 264, LANES), F32),
            pltpu.VMEM((NX, 256, LANES), F32),
            pltpu.VMEM((NX, 264, LANES), F32),
            pltpu.VMEM((NX, 2, 64, LANES), F32),
            pltpu.VMEM((16, 8, LANES), F32),
            pltpu.VMEM((NX, 2, 64, LANES), F32),
            pltpu.VMEM((320, 256), BF16),
            pltpu.VMEM((512, 256), F32),
            pltpu.VMEM((512, DOF), F32),
            pltpu.VMEM((576, 256), BF16),
            pltpu.VMEM((8, 128, 256), BF16),
            pltpu.VMEM((8, 192, 256), F32),
            pltpu.VMEM((16, 64, LANES), F32),
            pltpu.VMEM((NX, 2, 64, LANES), F32),
            pltpu.VMEM((NT, 16, LANES), F32),
            pltpu.VMEM((NT, 16, LANES), F32),
            pltpu.VMEM((NZ, 64, LANES), F32),
            pltpu.VMEM((NZ - 1, 64, LANES), F32),
            pltpu.VMEM((NT, 16, LANES), F32),
            pltpu.VMEM((NX, 2, 64, LANES), F32),
            pltpu.VMEM((NT, 16, LANES), F32),
            pltpu.VMEM((DOF, DOF), F32),
            pltpu.VMEM((4 * DOF, DOF), F32),
            pltpu.VMEM((DOF, DOF), F32),
            dma((6,)), dma((2,)), dma((2,)),
            dma((NX,)), dma((NX,)), dma((NX,)), dma((NX,)), dma((NX,)), dma((NX,)),
            dma, dma, dma((NX,)), dma((NX,)), dma, dma, pltpu.SemaphoreType.REGULAR,
        ],
        compiler_params=pltpu.CompilerParams(
            collective_id=0, has_side_effects=True, vmem_limit_bytes=24 * 1024 * 1024
        ),
    )(
        in_hbm(guesses.reshape(DOF * 8, LANES)), in_hbm(forcing.reshape(DOF * 8, LANES)), step_weight, in_hbm(land_mask),
        in_hbm(fine_matrix), in_hbm(coupling.reshape(4 * DOF, DOF)), in_hbm(coarse_matrix),
    )
    return updated.reshape(guesses.shape), residual.reshape(guesses.shape)


def solution(mesh):
    tiles = P("tm", None, "gx", "gy")
    return jax.shard_map(
        per_device,
        mesh=mesh,
        in_specs=(tiles, tiles, P(), P("gx", "gy"), P(), P(), P()),
        out_specs=(tiles, tiles),
        check_vma=False,
    )
```

```python
import functools

import jax
import jax.numpy as jnp
from jax import lax
from jax.experimental import pallas as pl
from jax.experimental.pallas import tpu as pltpu
from jax.sharding import PartitionSpec as P

MESH = pl.DeviceIdType.MESH
F32, BF16 = jnp.float32, jnp.bfloat16

NT, NZ, NY, NX = 32, 8, 4, 4
DOF, STEPS, LANES = 64, 16, 128
STRIP, HALO = 32, 16


def split(value):
    high = value.astype(BF16)
    return high, (value - high.astype(F32)).astype(BF16)


def right_operand(value):
    high, low = split(value)
    return jnp.concatenate([high, low, high, low], axis=0)


def left_operand(ref, rows, value, temporary):
    high = value.astype(BF16).astype(F32)
    low = value - high
    size = value.shape[0]
    for slot, part in enumerate((high, high, low, low)):
        temporary[0:size, 64 * slot : 64 * slot + 64] = part
    ref[rows, :] = temporary[0:size, :].astype(BF16)


def mul(left, right):
    return jnp.dot(left, right, preferred_element_type=F32)


def exact(left, right):
    return jnp.dot(left, right, precision=lax.Precision.HIGHEST, preferred_element_type=F32)


def kernel(
    g_hbm, f_hbm, weight, mask_hbm, fine_hbm, coupling_hbm, coarse_hbm,
    upd_v, res_v,
    gv, fv, g_edge, f_edge, mask_in, g_pack, f_pack, start, strip_f, strip_g, mask_s, g_dense,
    fine_op, temporary, powers, power_op, state, product, last, dense, packed, gathered, scan, sums,
    e_out, res_parts, e_parts,
    fine, coupling, coarse, load_sem, edge_send, edge_recv, start_send, start_recv, f_send, f_recv, g_send, g_recv,
    d_send, d_recv, r_send, r_recv, e_send, e_recv, group_sem,
):
    tm, gx, gy = lax.axis_index("tm"), lax.axis_index("gx"), lax.axis_index("gy")
    y, z = tm // NZ, lax.rem(tm, NZ)
    owner = lax.rem(z // 2 + NX - gx, NX)
    returns_here = owner == gx
    lane = lax.broadcasted_iota(jnp.int32, (64, LANES), 1)
    lane8 = lax.broadcasted_iota(jnp.int32, (8, LANES), 1)

    def remote(source, target, send, recv, device):
        return pltpu.make_async_remote_copy(
            src_ref=source, dst_ref=target, send_sem=send, recv_sem=recv, device_id=device, device_id_type=MESH
        )

    g_load = pltpu.make_async_copy(g_hbm, gv, load_sem.at[0])
    f_load = pltpu.make_async_copy(f_hbm, fv.at[pl.ds(0, 512)], load_sem.at[1])
    m_load = pltpu.make_async_copy(mask_hbm, mask_in, load_sem.at[2])
    g_load.start()
    m_load.start()
    f_load.start()
    matrix_loads = [
        pltpu.make_async_copy(source, target, load_sem.at[3 + n])
        for n, (source, target) in enumerate(((fine_hbm, fine), (coupling_hbm, coupling), (coarse_hbm, coarse)))
    ]
    for load in matrix_loads:
        load.start()

    barrier = pltpu.get_barrier_semaphore()

    def tell(device):
        pl.semaphore_signal(barrier, inc=1, device_id=device, device_id_type=MESH)

    later = lax.rem(tm + 1, NT)
    earlier = lax.rem(tm + NT - 1, NT)
    tell((tm, gx, 1 - gy))
    for q in range(NX):
        tell((later, q, gy))
    for d in range(1, NX):
        tell((tm, lax.rem(gx + d, NX), gy))
    for d in range(1, NZ):
        tell((y * NZ + lax.rem(z + d, NZ), gx, gy))
    for d in range(1, NY):
        tell((lax.rem(y + d, NY) * NZ + z, gx, gy))

    m_load.wait()
    fv[512:520, :] = mask_in[...].astype(F32)
    g_load.wait()
    f_load.wait()

    def window(low_row, high_row, q):
        begin = STRIP * q - HALO
        where = lane[: low_row.shape[0]]
        return jnp.where(
            where < 64, pltpu.roll(low_row, (-begin) % LANES, 1), pltpu.roll(high_row, (64 - begin) % LANES, 1)
        )

    has_low = (gy == 1).astype(F32)
    has_high = (gy == 0).astype(F32)

    def extended(own, edge, q):
        where = lane[: own.shape[0]]
        if q == 0:
            return jnp.where(where >= LANES - HALO, edge * has_low, own)
        if q == NX - 1:
            return jnp.where(where < HALO, edge * has_high, own)
        return own

    def row(ref, x):
        return ref[pl.ds(x, DOF, stride=8), :]

    def pack(own, edge, out, q):
        for i in range(4):
            parts = []
            for x in (i, i + 4):
                mine = row(own, x)
                parts.append(extended(mine, row(edge, x), q) if q in (0, NX - 1) else mine)
            out[q, 64 * i : 64 * i + 64, :] = window(parts[0], parts[1], q)

    def pack_mask(q):
        mine = fv[512:520, :]
        if q in (0, NX - 1):
            mine = extended(mine, f_edge[512:520, :], q)
        f_pack[q, 256:264, :] = window(mine, pltpu.roll(mine, 4, 0), q)

    g_swap = remote(gv, g_edge, edge_send.at[0], edge_recv.at[0], (tm, gx, 1 - gy))
    f_swap = remote(fv, f_edge, edge_send.at[1], edge_recv.at[1], (tm, gx, 1 - gy))

    def start_copy(q):
        return remote(g_pack.at[q], start.at[gx], start_send.at[q], start_recv.at[gx], (earlier, q, gy))

    def strip_copy(source, target, send, recv, q):
        return remote(source.at[q], target.at[gx], send.at[q], recv.at[gx], (tm, q, gy))

    def strip_send(source, target, send, recv, q):
        @pl.when(gx != q)
        def _():
            strip_copy(source, target, send, recv, q).start()

        @pl.when(gx == q)
        def _():
            pltpu.make_async_copy(source.at[q], target.at[gx], recv.at[gx]).start()

    def columns_copy(p):
        return remote(packed.at[p], gathered.at[tm], d_send, d_recv, (p, gx, gy))

    def e_copy(p):
        slot = (lax.rem(z, 2) * 4 + y) * NX + gx
        return remote(e_out.at[p], e_parts.at[slot], e_send, e_recv, (p, owner, gy))

    def finish():
        g_swap.wait_send()
        f_swap.wait_send()
        for q in range(NX):
            start_copy(q).wait_send()

            @pl.when(gx != q)
            def _():
                strip_copy(f_pack, strip_f, f_send, f_recv, q).wait_send()
                strip_copy(g_dense, strip_g, g_send, g_recv, q).wait_send()
        for q in range(NX):
            @pl.when(gx != q)
            def _():
                strip_copy(dense, res_parts, r_send, r_recv, q).wait_send()
        some = pl.ds(0, NT - 1)
        pltpu.make_async_copy(packed.at[some], gathered.at[some], d_send).wait()
        @pl.when(returns_here)
        def _():
            some = pl.ds(0, NT - 1)
            pltpu.make_async_copy(e_out.at[some], e_parts.at[some], e_send).wait()

        @pl.when(jnp.logical_not(returns_here))
        def _():
            pltpu.make_async_copy(e_out, e_parts, e_send).wait()

    for q in (1, 2):
        pack(gv, None, g_pack, q)
    pl.semaphore_wait(barrier, 18)
    for d in range(1, NY):
        pl.semaphore_signal(group_sem, inc=1, device_id=(lax.rem(y + d, NY) * NZ + z, gx, gy), device_id_type=MESH)
    g_swap.start()
    f_swap.start()
    qa = 1 + lax.rem(gx, 2)
    for q in (qa, 3 - qa):
        start_copy(q).start()
    g_swap.wait_recv()
    for q in (0, 3):
        pack(gv, g_edge, g_pack, q)
    qc = 3 * lax.rem(gx, 2)
    for q in (qc, 3 - qc):
        start_copy(q).start()
    for q in (1, 2):
        pack(fv, None, f_pack, q)
        pack_mask(q)
    f_swap.wait_recv()
    for q in (0, 3):
        pack(fv, f_edge, f_pack, q)
        pack_mask(q)
    for d in range(1, NX):
        strip_copy(f_pack, strip_f, f_send, f_recv, lax.rem(gx + d, NX)).start()
    pltpu.make_async_copy(f_pack.at[gx], strip_f.at[gx], f_recv.at[gx]).start()

    even_block = lax.rem(lane8 // STRIP, 2) == 0
    low_half = lane8 < 64

    def exchange(t):
        a = (
            jnp.where(low_half, t[0], pltpu.roll(t[2], 64, 1)),
            jnp.where(low_half, t[1], pltpu.roll(t[3], 64, 1)),
            jnp.where(low_half, pltpu.roll(t[0], 64, 1), t[2]),
            jnp.where(low_half, pltpu.roll(t[1], 64, 1), t[3]),
        )
        out = []
        for first, second in ((a[0], a[1]), (a[2], a[3])):
            out.append(jnp.where(even_block, first, pltpu.roll(second, STRIP, 1)))
            out.append(jnp.where(even_block, pltpu.roll(first, LANES - STRIP, 1), second))
        return out

    def place(h, b):
        return 2 * h + 4 * (b // 2) + b % 2

    for h in range(2):
        for v in range(8):
            rows = [
                gv[pl.ds(64 * v + place(h, b), 8, stride=8), :] * fv[512 + place(h, b) : 513 + place(h, b), :]
                for b in range(4)
            ]
            for q, tile in enumerate(exchange(rows)):
                g_dense[q, h, 8 * v : 8 * v + 8, :] = tile

    for load in matrix_loads:
        load.wait()
    left_operand(fine_op, pl.ds(0, 64), fine[...], temporary)
    left_operand(fine_op, pl.ds(64, 128), coupling[128:256, :], temporary)
    left_operand(fine_op, pl.ds(192, 128), coupling[0:128, :], temporary)
    c1 = coarse[...]
    powers[0:64, :] = c1
    c2 = exact(c1, c1)
    powers[64:128, :] = c2
    powers[128:256, :] = exact(powers[0:128, :], c2)
    powers[256:512, :] = exact(powers[0:256, :], powers[192:256, :])
    c8 = powers[448:512, :]
    c16 = exact(c8, c8)
    left_operand(power_op, pl.ds(0, 512), powers[...], temporary)
    left_operand(power_op, pl.ds(512, 64), c16, temporary)

    is_last_interval = tm == NT - 1
    for q in range(NX):
        remote(g_pack.at[q], start.at[q], start_send.at[q], start_recv.at[q], (earlier, q, gy)).wait_recv()
        for i in range(4):
            begin = jnp.where(is_last_interval, 0.0, start[q, 64 * i : 64 * i + 64, :])
            high, low = split(begin)
            pair, half = 2 * q + i // 2, LANES * (i % 2)
            state[pair, 0:64, half : half + LANES] = high
            state[pair, 64:128, half : half + LANES] = low
    for q in range(NX):
        remote(f_pack.at[q], strip_f.at[q], f_send.at[q], f_recv.at[q], (tm, q, gy)).wait_recv()
        for i in range(4):
            mask_s[4 * q + i] = jnp.broadcast_to(strip_f[q, 256 + i : 257 + i, :], (8, LANES))

    def part(q, i, kind):
        half = LANES * (i % 2)
        return product[2 * q + i // 2, 64 * kind : 64 * kind + 64, half : half + LANES]

    for d in range(1, NX):
        strip_copy(g_dense, strip_g, g_send, g_recv, lax.rem(gx + d, NX)).start()
    pltpu.make_async_copy(g_dense.at[gx], strip_g.at[gx], g_recv.at[gx]).start()

    def fine_step(k, final):
        scale = weight[k]
        low_lanes = lane < 64

        def multiply(pair):
            rows = state[pair]
            terms = mul(fine_op[:, 0:192], jnp.concatenate([rows, rows[0:64]], axis=0))
            for half in (slice(0, LANES), slice(LANES, 2 * LANES)):
                south = pltpu.roll(terms[64:128, half], 1, 1)
                north = pltpu.roll(terms[128:192, half], LANES - 1, 1)
                product[pair, 0:64, half] = terms[0:64, half] + (south + north)
            product[pair, 64:192] = terms[192:320]

        def combine(q):
            for i in range(4):
                if i > 0:
                    west = part(q, i - 1, 1)
                else:
                    before = part(q - 1, 3, 1) if q > 0 else jnp.zeros((64, LANES), F32)
                    west = pltpu.roll(jnp.where(low_lanes, part(q, 3, 1), before), 64, 1)
                if i < 3:
                    east = part(q, i + 1, 2)
                else:
                    after = part(q + 1, 0, 2) if q < NX - 1 else jnp.zeros((64, LANES), F32)
                    east = pltpu.roll(jnp.where(low_lanes, after, part(q, 0, 2)), 64, 1)
                value = (part(q, i, 0) + scale * strip_f[q, 64 * i : 64 * i + 64, :]) + (west + east)
                mask = mask_s[4 * q + i]
                value = (value.reshape(8, 8, LANES) * mask[None]).reshape(64, LANES)
                if final:
                    last[4 * q + i] = value
                else:
                    high, low = split(value)
                    pair, half = 2 * q + i // 2, LANES * (i % 2)
                    state[pair, 0:64, half : half + LANES] = high
                    state[pair, 64:128, half : half + LANES] = low

        for pair in range(8):
            multiply(pair)
            if pair % 2 == 0 and pair > 0:
                combine(pair // 2 - 1)
        combine(NX - 1)

    def body(step, carry):
        fine_step(STEPS - 1 - step, False)
        return carry

    lax.fori_loop(0, STEPS - 1, body, 0, unroll=5)
    fine_step(0, True)

    even_lanes = lax.rem(lane // STRIP, 2) == 0
    for q in range(NX):
        remote(g_dense.at[q], strip_g.at[q], g_send.at[q], g_recv.at[q], (tm, q, gy)).wait_recv()
        for h in range(2):
            tile = jnp.where(
                even_lanes, pltpu.roll(last[4 * q + 2 * h], LANES - HALO, 1), pltpu.roll(last[4 * q + 2 * h + 1], HALO, 1)
            ) - strip_g[q, h]
            dense[q, h] = tile
            for u in range(2):
                pieces = exchange([tile[8 * (2 * c + u) : 8 * (2 * c + u) + 8] for c in range(4)])
                for b in range(4):
                    packed[b * NZ + 2 * lax.rem(q + gx, NX) + h, 8 * u : 8 * u + 8, :] = pieces[b]

    pl.semaphore_wait(group_sem, NY - 1)
    pltpu.make_async_copy(packed.at[tm], gathered.at[tm], d_recv).start()

    def send_columns(i, carry):
        columns_copy(lax.rem(tm + i, NT)).start()
        return carry

    lax.fori_loop(1, NT, send_columns, 0)
    for d in range(1, NX):
        strip_copy(dense, res_parts, r_send, r_recv, lax.rem(gx + d, NX)).start()
    pltpu.make_async_copy(dense.at[gx], res_parts.at[gx], r_recv.at[gx]).start()

    pltpu.make_async_copy(packed, gathered, d_recv).wait()
    for k in range(NZ):
        for u in range(2):
            pieces = exchange([gathered[i * NZ + k, 8 * u : 8 * u + 8, :] for i in range(NY)])
            for c in range(4):
                scan[k, 8 * (2 * c + u) : 8 * (2 * c + u) + 8, :] = pieces[c]
    for k in range(1, NZ):
        terms = mul(power_op[0 : 64 * k, :], right_operand(scan[k]))
        for p in range(1, k + 1):
            scan_sum = terms[64 * (p - 1) : 64 * p, :]
            if p == k:
                sums[0] = (sums[0] if k > 1 else scan[0]) + scan_sum
            else:
                sums[k - p] = (sums[k - p] if p > 1 else scan[k - p]) + scan_sum
    total = sums[0]
    zero = jnp.zeros((64, LANES), F32)

    def from_later(d):
        return jnp.where(lane < LANES - STRIP * d, pltpu.roll(total, LANES - STRIP * d, 1), zero)

    entering = from_later(1) + mul(power_op[448:512, :], right_operand(from_later(2))) + mul(
        power_op[512:576, :], right_operand(from_later(3))
    )
    carried = mul(power_op[0:512, :], right_operand(entering))
    for k in range(NZ):
        local = sums[k] if k < NZ - 1 else scan[k]
        tile = local + carried[64 * (NZ - 1 - k) : 64 * (NZ - k), :]
        for u in range(2):
            pieces = exchange([tile[8 * (2 * c + u) : 8 * (2 * c + u) + 8] for c in range(4)])
            for i in range(NY):
                e_out[i * NZ + k, 8 * u : 8 * u + 8, :] = pieces[i]

    @pl.when(returns_here)
    def _():
        slot = (lax.rem(z, 2) * 4 + y) * NX + gx
        pltpu.make_async_copy(e_out.at[tm], e_parts.at[slot], e_recv).start()

    @pl.when(jnp.logical_not(returns_here))
    def _():
        e_copy(tm).start()

    def send_result(i, carry):
        e_copy(lax.rem(tm + i, NT)).start()
        return carry

    lax.fori_loop(1, NT, send_result, 0)

    for q in range(NX):
        remote(dense.at[q], res_parts.at[q], r_send.at[q], r_recv.at[q], (tm, q, gy)).wait_recv()
    for h in range(2):
        for v in range(8):
            tiles = exchange([res_parts[q, h, 8 * v : 8 * v + 8, :] for q in range(NX)])
            for b in range(4):
                res_v[pl.ds(64 * v + place(h, b), 8, stride=8), :] = tiles[b]

    pltpu.make_async_copy(e_out, e_parts, e_recv).wait()
    for h in range(2):
        for b in range(4):
            for u in range(2):
                tiles = exchange([e_parts[(4 * h + b) * NX + q, 8 * u : 8 * u + 8, :] for q in range(NX)])
                for c in range(4):
                    where = pl.ds(64 * (2 * c + u) + place(h, b), 8, stride=8)
                    upd_v[where, :] = gv[where, :] + tiles[c]

    finish()


def per_device(guesses, forcing, step_weight, land_mask, fine_matrix, coupling, coarse_matrix):
    vmem = pl.BlockSpec(memory_space=pltpu.VMEM)
    hbm = pl.BlockSpec(memory_space=pltpu.HBM)

    def in_hbm(value):
        return pltpu.with_memory_space_constraint(value, pltpu.HBM)

    flat = jax.ShapeDtypeStruct((DOF * 8, LANES), F32)
    dma = pltpu.SemaphoreType.DMA
    updated, residual = pl.pallas_call(
        kernel,
        out_shape=(flat, flat),
        in_specs=[hbm, hbm, pl.BlockSpec(memory_space=pltpu.SMEM), hbm, hbm, hbm, hbm],
        out_specs=(vmem, vmem),
        scratch_shapes=[
            pltpu.VMEM((512, LANES), F32),
            pltpu.VMEM((520, LANES), F32),
            pltpu.VMEM((512, LANES), F32),
            pltpu.VMEM((520, LANES), F32),
            pltpu.VMEM((8, LANES), jnp.int32),
            pltpu.VMEM((NX, 256, LANES), F32),
            pltpu.VMEM((NX, 264, LANES), F32),
            pltpu.VMEM((NX, 256, LANES), F32),
            pltpu.VMEM((NX, 264, LANES), F32),
            pltpu.VMEM((NX, 2, 64, LANES), F32),
            pltpu.VMEM((16, 8, LANES), F32),
            pltpu.VMEM((NX, 2, 64, LANES), F32),
            pltpu.VMEM((320, 256), BF16),
            pltpu.VMEM((512, 256), F32),
            pltpu.VMEM((512, DOF), F32),
            pltpu.VMEM((576, 256), BF16),
            pltpu.VMEM((8, 128, 256), BF16),
            pltpu.VMEM((8, 192, 256), F32),
            pltpu.VMEM((16, 64, LANES), F32),
            pltpu.VMEM((NX, 2, 64, LANES), F32),
            pltpu.VMEM((NT, 16, LANES), F32),
            pltpu.VMEM((NT, 16, LANES), F32),
            pltpu.VMEM((NZ, 64, LANES), F32),
            pltpu.VMEM((NZ - 1, 64, LANES), F32),
            pltpu.VMEM((NT, 16, LANES), F32),
            pltpu.VMEM((NX, 2, 64, LANES), F32),
            pltpu.VMEM((NT, 16, LANES), F32),
            pltpu.VMEM((DOF, DOF), F32),
            pltpu.VMEM((4 * DOF, DOF), F32),
            pltpu.VMEM((DOF, DOF), F32),
            dma((6,)), dma((2,)), dma((2,)),
            dma((NX,)), dma((NX,)), dma((NX,)), dma((NX,)), dma((NX,)), dma((NX,)),
            dma, dma, dma((NX,)), dma((NX,)), dma, dma, pltpu.SemaphoreType.REGULAR,
        ],
        compiler_params=pltpu.CompilerParams(
            collective_id=0, has_side_effects=True, vmem_limit_bytes=24 * 1024 * 1024
        ),
    )(
        in_hbm(guesses.reshape(DOF * 8, LANES)), in_hbm(forcing.reshape(DOF * 8, LANES)), step_weight, in_hbm(land_mask),
        in_hbm(fine_matrix), in_hbm(coupling.reshape(4 * DOF, DOF)), in_hbm(coarse_matrix),
    )
    return updated.reshape(guesses.shape), residual.reshape(guesses.shape)


def solution(mesh):
    tiles = P("tm", None, "gx", "gy")
    return jax.shard_map(
        per_device,
        mesh=mesh,
        in_specs=(tiles, tiles, P(), P("gx", "gy"), P(), P(), P()),
        out_specs=(tiles, tiles),
        check_vma=False,
    )
```

```python
import functools

import jax
import jax.numpy as jnp
from jax import lax
from jax.experimental import pallas as pl
from jax.experimental.pallas import tpu as pltpu
from jax.sharding import PartitionSpec as P

MESH = pl.DeviceIdType.MESH
F32, BF16 = jnp.float32, jnp.bfloat16

NT, NZ, NY, NX = 32, 8, 4, 4
DOF, STEPS, LANES = 64, 16, 128
STRIP, HALO = 32, 16


def split(value):
    high = value.astype(BF16)
    return high, (value - high.astype(F32)).astype(BF16)


def right_operand(value):
    high, low = split(value)
    return jnp.concatenate([high, low, high, low], axis=0)


def left_operand(ref, rows, value, temporary):
    high = value.astype(BF16).astype(F32)
    low = value - high
    size = value.shape[0]
    for slot, part in enumerate((high, high, low, low)):
        temporary[0:size, 64 * slot : 64 * slot + 64] = part
    ref[rows, :] = temporary[0:size, :].astype(BF16)


def mul(left, right):
    return jnp.dot(left, right, preferred_element_type=F32)


def exact(left, right):
    return jnp.dot(left, right, precision=lax.Precision.HIGHEST, preferred_element_type=F32)


def kernel(
    g_hbm, f_hbm, weight, mask_hbm, fine_hbm, coupling_hbm, coarse_hbm,
    upd_v, res_v,
    gv, fv, g_edge, f_edge, mask_in, g_pack, f_pack, start, strip_f, strip_g, mask_s, g_dense,
    fine_op, temporary, powers, power_op, state, product, last, dense, packed, gathered, scan, sums,
    e_out, res_parts, e_parts,
    fine, coupling, coarse, load_sem, edge_send, edge_recv, start_send, start_recv, f_send, f_recv, g_send, g_recv,
    d_send, d_recv, r_send, r_recv, e_send, e_recv, group_sem,
):
    tm, gx, gy = lax.axis_index("tm"), lax.axis_index("gx"), lax.axis_index("gy")
    y, z = tm // NZ, lax.rem(tm, NZ)
    owner = lax.rem(z // 2 + NX - gx, NX)
    returns_here = owner == gx
    lane = lax.broadcasted_iota(jnp.int32, (64, LANES), 1)
    lane8 = lax.broadcasted_iota(jnp.int32, (8, LANES), 1)

    def remote(source, target, send, recv, device):
        return pltpu.make_async_remote_copy(
            src_ref=source, dst_ref=target, send_sem=send, recv_sem=recv, device_id=device, device_id_type=MESH
        )

    g_load = pltpu.make_async_copy(g_hbm, gv, load_sem.at[0])
    f_load = pltpu.make_async_copy(f_hbm, fv.at[pl.ds(0, 512)], load_sem.at[1])
    m_load = pltpu.make_async_copy(mask_hbm, mask_in, load_sem.at[2])
    g_load.start()
    m_load.start()
    f_load.start()
    matrix_loads = [
        pltpu.make_async_copy(source, target, load_sem.at[3 + n])
        for n, (source, target) in enumerate(((fine_hbm, fine), (coupling_hbm, coupling), (coarse_hbm, coarse)))
    ]
    for load in matrix_loads:
        load.start()

    barrier = pltpu.get_barrier_semaphore()

    def tell(device):
        pl.semaphore_signal(barrier, inc=1, device_id=device, device_id_type=MESH)

    later = lax.rem(tm + 1, NT)
    earlier = lax.rem(tm + NT - 1, NT)
    tell((tm, gx, 1 - gy))
    for q in range(NX):
        tell((later, q, gy))
    for d in range(1, NX):
        tell((tm, lax.rem(gx + d, NX), gy))
    for d in range(1, NZ):
        tell((y * NZ + lax.rem(z + d, NZ), gx, gy))
    for d in range(1, NY):
        tell((lax.rem(y + d, NY) * NZ + z, gx, gy))

    m_load.wait()
    fv[512:520, :] = mask_in[...].astype(F32)
    g_load.wait()
    f_load.wait()

    def window(low_row, high_row, q):
        begin = STRIP * q - HALO
        where = lane[: low_row.shape[0]]
        return jnp.where(
            where < 64, pltpu.roll(low_row, (-begin) % LANES, 1), pltpu.roll(high_row, (64 - begin) % LANES, 1)
        )

    has_low = (gy == 1).astype(F32)
    has_high = (gy == 0).astype(F32)

    def extended(own, edge, q):
        where = lane[: own.shape[0]]
        if q == 0:
            return jnp.where(where >= LANES - HALO, edge * has_low, own)
        if q == NX - 1:
            return jnp.where(where < HALO, edge * has_high, own)
        return own

    def row(ref, x):
        return ref[pl.ds(x, DOF, stride=8), :]

    def pack(own, edge, out, q):
        for i in range(4):
            parts = []
            for x in (i, i + 4):
                mine = row(own, x)
                parts.append(extended(mine, row(edge, x), q) if q in (0, NX - 1) else mine)
            out[q, 64 * i : 64 * i + 64, :] = window(parts[0], parts[1], q)

    def pack_mask(q):
        mine = fv[512:520, :]
        if q in (0, NX - 1):
            mine = extended(mine, f_edge[512:520, :], q)
        f_pack[q, 256:264, :] = window(mine, pltpu.roll(mine, 4, 0), q)

    g_swap = remote(gv, g_edge, edge_send.at[0], edge_recv.at[0], (tm, gx, 1 - gy))
    f_swap = remote(fv, f_edge, edge_send.at[1], edge_recv.at[1], (tm, gx, 1 - gy))

    def start_copy(q):
        return remote(g_pack.at[q], start.at[gx], start_send.at[q], start_recv.at[gx], (earlier, q, gy))

    def strip_copy(source, target, send, recv, q):
        return remote(source.at[q], target.at[gx], send.at[q], recv.at[gx], (tm, q, gy))

    def strip_send(source, target, send, recv, q):
        @pl.when(gx != q)
        def _():
            strip_copy(source, target, send, recv, q).start()

        @pl.when(gx == q)
        def _():
            pltpu.make_async_copy(source.at[q], target.at[gx], recv.at[gx]).start()

    def columns_copy(p):
        return remote(packed.at[p], gathered.at[tm], d_send, d_recv, (p, gx, gy))

    def e_copy(p):
        slot = (lax.rem(z, 2) * 4 + y) * NX + gx
        return remote(e_out.at[p], e_parts.at[slot], e_send, e_recv, (p, owner, gy))

    def finish():
        g_swap.wait_send()
        f_swap.wait_send()
        for q in range(NX):
            start_copy(q).wait_send()

            @pl.when(gx != q)
            def _():
                strip_copy(f_pack, strip_f, f_send, f_recv, q).wait_send()
                strip_copy(g_dense, strip_g, g_send, g_recv, q).wait_send()
        for q in range(NX):
            @pl.when(gx != q)
            def _():
                strip_copy(dense, res_parts, r_send, r_recv, q).wait_send()
        some = pl.ds(0, NT - 1)
        pltpu.make_async_copy(packed.at[some], gathered.at[some], d_send).wait()
        @pl.when(returns_here)
        def _():
            some = pl.ds(0, NT - 1)
            pltpu.make_async_copy(e_out.at[some], e_parts.at[some], e_send).wait()

        @pl.when(jnp.logical_not(returns_here))
        def _():
            pltpu.make_async_copy(e_out, e_parts, e_send).wait()

    for q in (1, 2):
        pack(gv, None, g_pack, q)
    pl.semaphore_wait(barrier, 18)
    for d in range(1, NY):
        pl.semaphore_signal(group_sem, inc=1, device_id=(lax.rem(y + d, NY) * NZ + z, gx, gy), device_id_type=MESH)
    g_swap.start()
    f_swap.start()
    qa = 1 + lax.rem(gx, 2)
    for q in (qa, 3 - qa):
        start_copy(q).start()
    g_swap.wait_recv()
    for q in (0, 3):
        pack(gv, g_edge, g_pack, q)
    qc = 3 * lax.rem(gx, 2)
    for q in (qc, 3 - qc):
        start_copy(q).start()
    for q in (1, 2):
        pack(fv, None, f_pack, q)
        pack_mask(q)
    f_swap.wait_recv()
    for q in (0, 3):
        pack(fv, f_edge, f_pack, q)
        pack_mask(q)
    for d in range(1, NX):
        strip_copy(f_pack, strip_f, f_send, f_recv, lax.rem(gx + d, NX)).start()
    pltpu.make_async_copy(f_pack.at[gx], strip_f.at[gx], f_recv.at[gx]).start()

    even_block = lax.rem(lane8 // STRIP, 2) == 0
    low_half = lane8 < 64

    def exchange(t):
        a = (
            jnp.where(low_half, t[0], pltpu.roll(t[2], 64, 1)),
            jnp.where(low_half, t[1], pltpu.roll(t[3], 64, 1)),
            jnp.where(low_half, pltpu.roll(t[0], 64, 1), t[2]),
            jnp.where(low_half, pltpu.roll(t[1], 64, 1), t[3]),
        )
        out = []
        for first, second in ((a[0], a[1]), (a[2], a[3])):
            out.append(jnp.where(even_block, first, pltpu.roll(second, STRIP, 1)))
            out.append(jnp.where(even_block, pltpu.roll(first, LANES - STRIP, 1), second))
        return out

    def place(h, b):
        return 2 * h + 4 * (b // 2) + b % 2

    for h in range(2):
        for v in range(8):
            rows = [
                gv[pl.ds(64 * v + place(h, b), 8, stride=8), :] * fv[512 + place(h, b) : 513 + place(h, b), :]
                for b in range(4)
            ]
            for q, tile in enumerate(exchange(rows)):
                g_dense[q, h, 8 * v : 8 * v + 8, :] = tile

    for load in matrix_loads:
        load.wait()
    left_operand(fine_op, pl.ds(0, 64), fine[...], temporary)
    left_operand(fine_op, pl.ds(64, 128), coupling[128:256, :], temporary)
    left_operand(fine_op, pl.ds(192, 128), coupling[0:128, :], temporary)
    c1 = coarse[...]
    powers[0:64, :] = c1
    c2 = exact(c1, c1)
    powers[64:128, :] = c2
    powers[128:256, :] = exact(powers[0:128, :], c2)
    powers[256:512, :] = exact(powers[0:256, :], powers[192:256, :])
    c8 = powers[448:512, :]
    c16 = exact(c8, c8)
    left_operand(power_op, pl.ds(0, 512), powers[...], temporary)
    left_operand(power_op, pl.ds(512, 64), c16, temporary)

    is_last_interval = tm == NT - 1
    for q in range(NX):
        remote(g_pack.at[q], start.at[q], start_send.at[q], start_recv.at[q], (earlier, q, gy)).wait_recv()
        for i in range(4):
            begin = jnp.where(is_last_interval, 0.0, start[q, 64 * i : 64 * i + 64, :])
            high, low = split(begin)
            pair, half = 2 * q + i // 2, LANES * (i % 2)
            state[pair, 0:64, half : half + LANES] = high
            state[pair, 64:128, half : half + LANES] = low
    for q in range(NX):
        remote(f_pack.at[q], strip_f.at[q], f_send.at[q], f_recv.at[q], (tm, q, gy)).wait_recv()
        for i in range(4):
            mask_s[4 * q + i] = jnp.broadcast_to(strip_f[q, 256 + i : 257 + i, :], (8, LANES))

    def part(q, i, kind):
        half = LANES * (i % 2)
        return product[2 * q + i // 2, 64 * kind : 64 * kind + 64, half : half + LANES]

    for d in range(1, NX):
        strip_copy(g_dense, strip_g, g_send, g_recv, lax.rem(gx + d, NX)).start()
    pltpu.make_async_copy(g_dense.at[gx], strip_g.at[gx], g_recv.at[gx]).start()

    def fine_step(k, final):
        scale = weight[k]
        low_lanes = lane < 64

        def multiply(pair):
            rows = state[pair]
            terms = mul(fine_op[:, 0:192], jnp.concatenate([rows, rows[0:64]], axis=0))
            for half in (slice(0, LANES), slice(LANES, 2 * LANES)):
                south = pltpu.roll(terms[64:128, half], 1, 1)
                north = pltpu.roll(terms[128:192, half], LANES - 1, 1)
                product[pair, 0:64, half] = terms[0:64, half] + (south + north)
            product[pair, 64:192] = terms[192:320]

        def combine(q):
            for i in range(4):
                if i > 0:
                    west = part(q, i - 1, 1)
                else:
                    before = part(q - 1, 3, 1) if q > 0 else jnp.zeros((64, LANES), F32)
                    west = pltpu.roll(jnp.where(low_lanes, part(q, 3, 1), before), 64, 1)
                if i < 3:
                    east = part(q, i + 1, 2)
                else:
                    after = part(q + 1, 0, 2) if q < NX - 1 else jnp.zeros((64, LANES), F32)
                    east = pltpu.roll(jnp.where(low_lanes, after, part(q, 0, 2)), 64, 1)
                value = (part(q, i, 0) + scale * strip_f[q, 64 * i : 64 * i + 64, :]) + (west + east)
                mask = mask_s[4 * q + i]
                value = (value.reshape(8, 8, LANES) * mask[None]).reshape(64, LANES)
                if final:
                    last[4 * q + i] = value
                else:
                    high, low = split(value)
                    pair, half = 2 * q + i // 2, LANES * (i % 2)
                    state[pair, 0:64, half : half + LANES] = high
                    state[pair, 64:128, half : half + LANES] = low

        for pair in range(8):
            multiply(pair)
            if pair % 2 == 0 and pair > 0:
                combine(pair // 2 - 1)
        combine(NX - 1)

    def body(step, carry):
        fine_step(STEPS - 1 - step, False)
        return carry

    lax.fori_loop(0, STEPS - 1, body, 0, unroll=15)
    fine_step(0, True)

    even_lanes = lax.rem(lane // STRIP, 2) == 0
    for q in range(NX):
        remote(g_dense.at[q], strip_g.at[q], g_send.at[q], g_recv.at[q], (tm, q, gy)).wait_recv()
        for h in range(2):
            tile = jnp.where(
                even_lanes, pltpu.roll(last[4 * q + 2 * h], LANES - HALO, 1), pltpu.roll(last[4 * q + 2 * h + 1], HALO, 1)
            ) - strip_g[q, h]
            dense[q, h] = tile
            for u in range(2):
                pieces = exchange([tile[8 * (2 * c + u) : 8 * (2 * c + u) + 8] for c in range(4)])
                for b in range(4):
                    packed[b * NZ + 2 * lax.rem(q + gx, NX) + h, 8 * u : 8 * u + 8, :] = pieces[b]

    pl.semaphore_wait(group_sem, NY - 1)
    pltpu.make_async_copy(packed.at[tm], gathered.at[tm], d_recv).start()

    def send_columns(i, carry):
        columns_copy(lax.rem(tm + i, NT)).start()
        return carry

    lax.fori_loop(1, NT, send_columns, 0)
    for d in range(1, NX):
        strip_copy(dense, res_parts, r_send, r_recv, lax.rem(gx + d, NX)).start()
    pltpu.make_async_copy(dense.at[gx], res_parts.at[gx], r_recv.at[gx]).start()

    pltpu.make_async_copy(packed, gathered, d_recv).wait()
    for k in range(NZ):
        for u in range(2):
            pieces = exchange([gathered[i * NZ + k, 8 * u : 8 * u + 8, :] for i in range(NY)])
            for c in range(4):
                scan[k, 8 * (2 * c + u) : 8 * (2 * c + u) + 8, :] = pieces[c]
    for k in range(1, NZ):
        terms = mul(power_op[0 : 64 * k, :], right_operand(scan[k]))
        for p in range(1, k + 1):
            scan_sum = terms[64 * (p - 1) : 64 * p, :]
            if p == k:
                sums[0] = (sums[0] if k > 1 else scan[0]) + scan_sum
            else:
                sums[k - p] = (sums[k - p] if p > 1 else scan[k - p]) + scan_sum
    total = sums[0]
    zero = jnp.zeros((64, LANES), F32)

    def from_later(d):
        return jnp.where(lane < LANES - STRIP * d, pltpu.roll(total, LANES - STRIP * d, 1), zero)

    entering = from_later(1) + mul(power_op[448:512, :], right_operand(from_later(2))) + mul(
        power_op[512:576, :], right_operand(from_later(3))
    )
    carried = mul(power_op[0:512, :], right_operand(entering))
    for k in range(NZ):
        local = sums[k] if k < NZ - 1 else scan[k]
        tile = local + carried[64 * (NZ - 1 - k) : 64 * (NZ - k), :]
        for u in range(2):
            pieces = exchange([tile[8 * (2 * c + u) : 8 * (2 * c + u) + 8] for c in range(4)])
            for i in range(NY):
                e_out[i * NZ + k, 8 * u : 8 * u + 8, :] = pieces[i]

    @pl.when(returns_here)
    def _():
        slot = (lax.rem(z, 2) * 4 + y) * NX + gx
        pltpu.make_async_copy(e_out.at[tm], e_parts.at[slot], e_recv).start()

    @pl.when(jnp.logical_not(returns_here))
    def _():
        e_copy(tm).start()

    def send_result(i, carry):
        e_copy(lax.rem(tm + i, NT)).start()
        return carry

    lax.fori_loop(1, NT, send_result, 0)

    for q in range(NX):
        remote(dense.at[q], res_parts.at[q], r_send.at[q], r_recv.at[q], (tm, q, gy)).wait_recv()
    for h in range(2):
        for v in range(8):
            tiles = exchange([res_parts[q, h, 8 * v : 8 * v + 8, :] for q in range(NX)])
            for b in range(4):
                res_v[pl.ds(64 * v + place(h, b), 8, stride=8), :] = tiles[b]

    pltpu.make_async_copy(e_out, e_parts, e_recv).wait()
    for h in range(2):
        for b in range(4):
            for u in range(2):
                tiles = exchange([e_parts[(4 * h + b) * NX + q, 8 * u : 8 * u + 8, :] for q in range(NX)])
                for c in range(4):
                    where = pl.ds(64 * (2 * c + u) + place(h, b), 8, stride=8)
                    upd_v[where, :] = gv[where, :] + tiles[c]

    finish()


def per_device(guesses, forcing, step_weight, land_mask, fine_matrix, coupling, coarse_matrix):
    vmem = pl.BlockSpec(memory_space=pltpu.VMEM)
    hbm = pl.BlockSpec(memory_space=pltpu.HBM)

    def in_hbm(value):
        return pltpu.with_memory_space_constraint(value, pltpu.HBM)

    flat = jax.ShapeDtypeStruct((DOF * 8, LANES), F32)
    dma = pltpu.SemaphoreType.DMA
    updated, residual = pl.pallas_call(
        kernel,
        out_shape=(flat, flat),
        in_specs=[hbm, hbm, pl.BlockSpec(memory_space=pltpu.SMEM), hbm, hbm, hbm, hbm],
        out_specs=(vmem, vmem),
        scratch_shapes=[
            pltpu.VMEM((512, LANES), F32),
            pltpu.VMEM((520, LANES), F32),
            pltpu.VMEM((512, LANES), F32),
            pltpu.VMEM((520, LANES), F32),
            pltpu.VMEM((8, LANES), jnp.int32),
            pltpu.VMEM((NX, 256, LANES), F32),
            pltpu.VMEM((NX, 264, LANES), F32),
            pltpu.VMEM((NX, 256, LANES), F32),
            pltpu.VMEM((NX, 264, LANES), F32),
            pltpu.VMEM((NX, 2, 64, LANES), F32),
            pltpu.VMEM((16, 8, LANES), F32),
            pltpu.VMEM((NX, 2, 64, LANES), F32),
            pltpu.VMEM((320, 256), BF16),
            pltpu.VMEM((512, 256), F32),
            pltpu.VMEM((512, DOF), F32),
            pltpu.VMEM((576, 256), BF16),
            pltpu.VMEM((8, 128, 256), BF16),
            pltpu.VMEM((8, 192, 256), F32),
            pltpu.VMEM((16, 64, LANES), F32),
            pltpu.VMEM((NX, 2, 64, LANES), F32),
            pltpu.VMEM((NT, 16, LANES), F32),
            pltpu.VMEM((NT, 16, LANES), F32),
            pltpu.VMEM((NZ, 64, LANES), F32),
            pltpu.VMEM((NZ - 1, 64, LANES), F32),
            pltpu.VMEM((NT, 16, LANES), F32),
            pltpu.VMEM((NX, 2, 64, LANES), F32),
            pltpu.VMEM((NT, 16, LANES), F32),
            pltpu.VMEM((DOF, DOF), F32),
            pltpu.VMEM((4 * DOF, DOF), F32),
            pltpu.VMEM((DOF, DOF), F32),
            dma((6,)), dma((2,)), dma((2,)),
            dma((NX,)), dma((NX,)), dma((NX,)), dma((NX,)), dma((NX,)), dma((NX,)),
            dma, dma, dma((NX,)), dma((NX,)), dma, dma, pltpu.SemaphoreType.REGULAR,
        ],
        compiler_params=pltpu.CompilerParams(
            collective_id=0, has_side_effects=True, vmem_limit_bytes=24 * 1024 * 1024
        ),
    )(
        in_hbm(guesses.reshape(DOF * 8, LANES)), in_hbm(forcing.reshape(DOF * 8, LANES)), step_weight, in_hbm(land_mask),
        in_hbm(fine_matrix), in_hbm(coupling.reshape(4 * DOF, DOF)), in_hbm(coarse_matrix),
    )
    return updated.reshape(guesses.shape), residual.reshape(guesses.shape)


def solution(mesh):
    tiles = P("tm", None, "gx", "gy")
    return jax.shard_map(
        per_device,
        mesh=mesh,
        in_specs=(tiles, tiles, P(), P("gx", "gy"), P(), P(), P()),
        out_specs=(tiles, tiles),
        check_vma=False,
    )
```

```python
import functools

import jax
import jax.numpy as jnp
from jax import lax
from jax.experimental import pallas as pl
from jax.experimental.pallas import tpu as pltpu
from jax.sharding import PartitionSpec as P

MESH = pl.DeviceIdType.MESH
F32, BF16 = jnp.float32, jnp.bfloat16

NT, NZ, NY, NX = 32, 8, 4, 4
DOF, STEPS, LANES = 64, 16, 128
STRIP, HALO = 32, 16


def split(value):
    high = value.astype(BF16)
    return high, (value - high.astype(F32)).astype(BF16)


def right_operand(value):
    high, low = split(value)
    return jnp.concatenate([high, low, high, low], axis=0)


def left_operand(ref, rows, value, temporary):
    high = value.astype(BF16).astype(F32)
    low = value - high
    size = value.shape[0]
    for slot, part in enumerate((high, high, low, low)):
        temporary[0:size, 64 * slot : 64 * slot + 64] = part
    ref[rows, :] = temporary[0:size, :].astype(BF16)


def mul(left, right):
    return jnp.dot(left, right, preferred_element_type=F32)


def exact(left, right):
    return jnp.dot(left, right, precision=lax.Precision.HIGHEST, preferred_element_type=F32)


def kernel(
    g_hbm, f_hbm, weight, mask_hbm, fine_hbm, coupling_hbm, coarse_hbm,
    upd_v, res_v,
    gv, fv, g_edge, f_edge, mask_in, g_pack, f_pack, start, strip_f, strip_g, mask_s, g_dense,
    fine_op, temporary, powers, power_op, state, product, last, dense, packed, gathered, scan, sums,
    e_out, res_parts, e_parts,
    fine, coupling, coarse, load_sem, edge_send, edge_recv, start_send, start_recv, f_send, f_recv, g_send, g_recv,
    d_send, d_recv, r_send, r_recv, e_send, e_recv, group_sem,
):
    tm, gx, gy = lax.axis_index("tm"), lax.axis_index("gx"), lax.axis_index("gy")
    y, z = tm // NZ, lax.rem(tm, NZ)
    owner = lax.rem(z // 2 + NX - gx, NX)
    returns_here = owner == gx
    lane = lax.broadcasted_iota(jnp.int32, (64, LANES), 1)
    lane8 = lax.broadcasted_iota(jnp.int32, (8, LANES), 1)

    def remote(source, target, send, recv, device):
        return pltpu.make_async_remote_copy(
            src_ref=source, dst_ref=target, send_sem=send, recv_sem=recv, device_id=device, device_id_type=MESH
        )

    g_load = pltpu.make_async_copy(g_hbm, gv, load_sem.at[0])
    f_load = pltpu.make_async_copy(f_hbm, fv.at[pl.ds(0, 512)], load_sem.at[1])
    m_load = pltpu.make_async_copy(mask_hbm, mask_in, load_sem.at[2])
    g_load.start()
    m_load.start()
    f_load.start()
    matrix_loads = [
        pltpu.make_async_copy(source, target, load_sem.at[3 + n])
        for n, (source, target) in enumerate(((fine_hbm, fine), (coupling_hbm, coupling), (coarse_hbm, coarse)))
    ]
    for load in matrix_loads:
        load.start()

    barrier = pltpu.get_barrier_semaphore()

    def tell(device):
        pl.semaphore_signal(barrier, inc=1, device_id=device, device_id_type=MESH)

    later = lax.rem(tm + 1, NT)
    earlier = lax.rem(tm + NT - 1, NT)
    tell((tm, gx, 1 - gy))
    for q in range(NX):
        tell((later, q, gy))
    for d in range(1, NX):
        tell((tm, lax.rem(gx + d, NX), gy))
    for d in range(1, NZ):
        tell((y * NZ + lax.rem(z + d, NZ), gx, gy))
    for d in range(1, NY):
        tell((lax.rem(y + d, NY) * NZ + z, gx, gy))

    m_load.wait()
    fv[512:520, :] = mask_in[...].astype(F32)
    g_load.wait()
    f_load.wait()

    def window(low_row, high_row, q):
        begin = STRIP * q - HALO
        where = lane[: low_row.shape[0]]
        return jnp.where(
            where < 64, pltpu.roll(low_row, (-begin) % LANES, 1), pltpu.roll(high_row, (64 - begin) % LANES, 1)
        )

    has_low = (gy == 1).astype(F32)
    has_high = (gy == 0).astype(F32)

    def extended(own, edge, q):
        where = lane[: own.shape[0]]
        if q == 0:
            return jnp.where(where >= LANES - HALO, edge * has_low, own)
        if q == NX - 1:
            return jnp.where(where < HALO, edge * has_high, own)
        return own

    def row(ref, x):
        return ref[pl.ds(x, DOF, stride=8), :]

    def pack(own, edge, out, q):
        for i in range(4):
            parts = []
            for x in (i, i + 4):
                mine = row(own, x)
                parts.append(extended(mine, row(edge, x), q) if q in (0, NX - 1) else mine)
            out[q, 64 * i : 64 * i + 64, :] = window(parts[0], parts[1], q)

    def pack_mask(q):
        mine = fv[512:520, :]
        if q in (0, NX - 1):
            mine = extended(mine, f_edge[512:520, :], q)
        f_pack[q, 256:264, :] = window(mine, pltpu.roll(mine, 4, 0), q)

    g_swap = remote(gv, g_edge, edge_send.at[0], edge_recv.at[0], (tm, gx, 1 - gy))
    f_swap = remote(fv, f_edge, edge_send.at[1], edge_recv.at[1], (tm, gx, 1 - gy))

    def start_copy(q):
        return remote(g_pack.at[q], start.at[gx], start_send.at[q], start_recv.at[gx], (earlier, q, gy))

    def strip_copy(source, target, send, recv, q):
        return remote(source.at[q], target.at[gx], send.at[q], recv.at[gx], (tm, q, gy))

    def strip_send(source, target, send, recv, q):
        @pl.when(gx != q)
        def _():
            strip_copy(source, target, send, recv, q).start()

        @pl.when(gx == q)
        def _():
            pltpu.make_async_copy(source.at[q], target.at[gx], recv.at[gx]).start()

    def columns_copy(p):
        return remote(packed.at[p], gathered.at[tm], d_send, d_recv, (p, gx, gy))

    def e_copy(p):
        slot = (lax.rem(z, 2) * 4 + y) * NX + gx
        return remote(e_out.at[p], e_parts.at[slot], e_send, e_recv, (p, owner, gy))

    def finish():
        g_swap.wait_send()
        f_swap.wait_send()
        for q in range(NX):
            start_copy(q).wait_send()

            @pl.when(gx != q)
            def _():
                strip_copy(f_pack, strip_f, f_send, f_recv, q).wait_send()
                strip_copy(g_dense, strip_g, g_send, g_recv, q).wait_send()
        for q in range(NX):
            @pl.when(gx != q)
            def _():
                strip_copy(dense, res_parts, r_send, r_recv, q).wait_send()
        some = pl.ds(0, NT - 1)
        pltpu.make_async_copy(packed.at[some], gathered.at[some], d_send).wait()
        @pl.when(returns_here)
        def _():
            some = pl.ds(0, NT - 1)
            pltpu.make_async_copy(e_out.at[some], e_parts.at[some], e_send).wait()

        @pl.when(jnp.logical_not(returns_here))
        def _():
            pltpu.make_async_copy(e_out, e_parts, e_send).wait()

    for q in (1, 2):
        pack(gv, None, g_pack, q)
    pl.semaphore_wait(barrier, 18)
    for d in range(1, NY):
        pl.semaphore_signal(group_sem, inc=1, device_id=(lax.rem(y + d, NY) * NZ + z, gx, gy), device_id_type=MESH)
    g_swap.start()
    f_swap.start()
    qa = 1 + lax.rem(gx, 2)
    for q in (qa, 3 - qa):
        start_copy(q).start()
    g_swap.wait_recv()
    for q in (0, 3):
        pack(gv, g_edge, g_pack, q)
    qc = 3 * lax.rem(gx, 2)
    for q in (qc, 3 - qc):
        start_copy(q).start()
    for q in (1, 2):
        pack(fv, None, f_pack, q)
        pack_mask(q)
    f_swap.wait_recv()
    for q in (0, 3):
        pack(fv, f_edge, f_pack, q)
        pack_mask(q)
    for d in range(1, NX):
        strip_copy(f_pack, strip_f, f_send, f_recv, lax.rem(gx + d, NX)).start()
    pltpu.make_async_copy(f_pack.at[gx], strip_f.at[gx], f_recv.at[gx]).start()

    even_block = lax.rem(lane8 // STRIP, 2) == 0
    low_half = lane8 < 64

    def exchange(t):
        a = (
            jnp.where(low_half, t[0], pltpu.roll(t[2], 64, 1)),
            jnp.where(low_half, t[1], pltpu.roll(t[3], 64, 1)),
            jnp.where(low_half, pltpu.roll(t[0], 64, 1), t[2]),
            jnp.where(low_half, pltpu.roll(t[1], 64, 1), t[3]),
        )
        out = []
        for first, second in ((a[0], a[1]), (a[2], a[3])):
            out.append(jnp.where(even_block, first, pltpu.roll(second, STRIP, 1)))
            out.append(jnp.where(even_block, pltpu.roll(first, LANES - STRIP, 1), second))
        return out

    def place(h, b):
        return 2 * h + 4 * (b // 2) + b % 2

    for h in range(2):
        for v in range(8):
            rows = [
                gv[pl.ds(64 * v + place(h, b), 8, stride=8), :] * fv[512 + place(h, b) : 513 + place(h, b), :]
                for b in range(4)
            ]
            for q, tile in enumerate(exchange(rows)):
                g_dense[q, h, 8 * v : 8 * v + 8, :] = tile

    for load in matrix_loads:
        load.wait()
    left_operand(fine_op, pl.ds(0, 64), fine[...], temporary)
    left_operand(fine_op, pl.ds(64, 128), coupling[128:256, :], temporary)
    left_operand(fine_op, pl.ds(192, 128), coupling[0:128, :], temporary)
    c1 = coarse[...]
    powers[0:64, :] = c1
    c2 = exact(c1, c1)
    powers[64:128, :] = c2
    powers[128:256, :] = exact(powers[0:128, :], c2)
    powers[256:512, :] = exact(powers[0:256, :], powers[192:256, :])
    c8 = powers[448:512, :]
    c16 = exact(c8, c8)
    left_operand(power_op, pl.ds(0, 512), powers[...], temporary)
    left_operand(power_op, pl.ds(512, 64), c16, temporary)

    is_last_interval = tm == NT - 1
    for q in range(NX):
        remote(g_pack.at[q], start.at[q], start_send.at[q], start_recv.at[q], (earlier, q, gy)).wait_recv()
        for i in range(4):
            begin = jnp.where(is_last_interval, 0.0, start[q, 64 * i : 64 * i + 64, :])
            high, low = split(begin)
            pair, half = 2 * q + i // 2, LANES * (i % 2)
            state[pair, 0:64, half : half + LANES] = high
            state[pair, 64:128, half : half + LANES] = low
    for q in range(NX):
        remote(f_pack.at[q], strip_f.at[q], f_send.at[q], f_recv.at[q], (tm, q, gy)).wait_recv()
        for i in range(4):
            mask_s[4 * q + i] = jnp.broadcast_to(strip_f[q, 256 + i : 257 + i, :], (8, LANES))

    def part(q, i, kind):
        half = LANES * (i % 2)
        return product[2 * q + i // 2, 64 * kind : 64 * kind + 64, half : half + LANES]

    for d in range(1, NX):
        strip_copy(g_dense, strip_g, g_send, g_recv, lax.rem(gx + d, NX)).start()
    pltpu.make_async_copy(g_dense.at[gx], strip_g.at[gx], g_recv.at[gx]).start()

    def fine_step(k, final):
        scale = weight[k]
        low_lanes = lane < 64

        def multiply(pair):
            rows = state[pair]
            terms = mul(fine_op[:, 0:192], jnp.concatenate([rows, rows[0:64]], axis=0))
            for half in (slice(0, LANES), slice(LANES, 2 * LANES)):
                south = pltpu.roll(terms[64:128, half], 1, 1)
                north = pltpu.roll(terms[128:192, half], LANES - 1, 1)
                product[pair, 0:64, half] = terms[0:64, half] + (south + north)
            product[pair, 64:192] = terms[192:320]

        def combine(q):
            for i in range(4):
                if i > 0:
                    west = part(q, i - 1, 1)
                else:
                    before = part(q - 1, 3, 1) if q > 0 else jnp.zeros((64, LANES), F32)
                    west = pltpu.roll(jnp.where(low_lanes, part(q, 3, 1), before), 64, 1)
                if i < 3:
                    east = part(q, i + 1, 2)
                else:
                    after = part(q + 1, 0, 2) if q < NX - 1 else jnp.zeros((64, LANES), F32)
                    east = pltpu.roll(jnp.where(low_lanes, after, part(q, 0, 2)), 64, 1)
                value = (part(q, i, 0) + scale * strip_f[q, 64 * i : 64 * i + 64, :]) + (west + east)
                mask = mask_s[4 * q + i]
                value = (value.reshape(8, 8, LANES) * mask[None]).reshape(64, LANES)
                if final:
                    last[4 * q + i] = value
                else:
                    high, low = split(value)
                    pair, half = 2 * q + i // 2, LANES * (i % 2)
                    state[pair, 0:64, half : half + LANES] = high
                    state[pair, 64:128, half : half + LANES] = low

        for pair in range(8):
            multiply(pair)
            if pair % 2 == 0 and pair > 0:
                combine(pair // 2 - 1)
        combine(NX - 1)

    def body(step, carry):
        fine_step(STEPS - 1 - step, False)
        return carry

    lax.fori_loop(0, STEPS - 1, body, 0, unroll=15)
    fine_step(0, True)

    even_lanes = lax.rem(lane // STRIP, 2) == 0
    pl.semaphore_wait(group_sem, NY - 1)
    for q in range(NX):
        remote(g_dense.at[q], strip_g.at[q], g_send.at[q], g_recv.at[q], (tm, q, gy)).wait_recv()
    for n in (4, 3, 5, 2, 6, 1, 7, 0):
        k = lax.rem(z + n, NZ)
        q, h = lax.rem(k // 2 + NX - gx, NX), lax.rem(k, 2)
        tile = jnp.where(
            even_lanes, pltpu.roll(last[4 * q + 2 * h], LANES - HALO, 1), pltpu.roll(last[4 * q + 2 * h + 1], HALO, 1)
        ) - strip_g[q, h]
        dense[q, h] = tile
        for u in range(2):
            pieces = exchange([tile[8 * (2 * c + u) : 8 * (2 * c + u) + 8] for c in range(4)])
            for b in range(4):
                packed[b * NZ + k, 8 * u : 8 * u + 8, :] = pieces[b]
        for b in range(4):
            p = lax.rem(y + b, NY) * NZ + k
            if b == 0 and n == 0:
                pltpu.make_async_copy(packed.at[tm], gathered.at[tm], d_recv).start()
            else:
                columns_copy(p).start()

    for d in range(1, NX):
        strip_copy(dense, res_parts, r_send, r_recv, lax.rem(gx + d, NX)).start()
    pltpu.make_async_copy(dense.at[gx], res_parts.at[gx], r_recv.at[gx]).start()

    pltpu.make_async_copy(packed, gathered, d_recv).wait()
    for k in range(NZ):
        for u in range(2):
            pieces = exchange([gathered[i * NZ + k, 8 * u : 8 * u + 8, :] for i in range(NY)])
            for c in range(4):
                scan[k, 8 * (2 * c + u) : 8 * (2 * c + u) + 8, :] = pieces[c]
    for k in range(1, NZ):
        terms = mul(power_op[0 : 64 * k, :], right_operand(scan[k]))
        for p in range(1, k + 1):
            scan_sum = terms[64 * (p - 1) : 64 * p, :]
            if p == k:
                sums[0] = (sums[0] if k > 1 else scan[0]) + scan_sum
            else:
                sums[k - p] = (sums[k - p] if p > 1 else scan[k - p]) + scan_sum
    total = sums[0]
    zero = jnp.zeros((64, LANES), F32)

    def from_later(d):
        return jnp.where(lane < LANES - STRIP * d, pltpu.roll(total, LANES - STRIP * d, 1), zero)

    entering = from_later(1) + mul(power_op[448:512, :], right_operand(from_later(2))) + mul(
        power_op[512:576, :], right_operand(from_later(3))
    )
    carried = mul(power_op[0:512, :], right_operand(entering))
    for k in range(NZ):
        local = sums[k] if k < NZ - 1 else scan[k]
        tile = local + carried[64 * (NZ - 1 - k) : 64 * (NZ - k), :]
        for u in range(2):
            pieces = exchange([tile[8 * (2 * c + u) : 8 * (2 * c + u) + 8] for c in range(4)])
            for i in range(NY):
                e_out[i * NZ + k, 8 * u : 8 * u + 8, :] = pieces[i]

    @pl.when(returns_here)
    def _():
        slot = (lax.rem(z, 2) * 4 + y) * NX + gx
        pltpu.make_async_copy(e_out.at[tm], e_parts.at[slot], e_recv).start()

    @pl.when(jnp.logical_not(returns_here))
    def _():
        e_copy(tm).start()

    def send_result(i, carry):
        e_copy(lax.rem(tm + i, NT)).start()
        return carry

    lax.fori_loop(1, NT, send_result, 0)

    for q in range(NX):
        remote(dense.at[q], res_parts.at[q], r_send.at[q], r_recv.at[q], (tm, q, gy)).wait_recv()
    for h in range(2):
        for v in range(8):
            tiles = exchange([res_parts[q, h, 8 * v : 8 * v + 8, :] for q in range(NX)])
            for b in range(4):
                res_v[pl.ds(64 * v + place(h, b), 8, stride=8), :] = tiles[b]

    pltpu.make_async_copy(e_out, e_parts, e_recv).wait()
    for h in range(2):
        for b in range(4):
            for u in range(2):
                tiles = exchange([e_parts[(4 * h + b) * NX + q, 8 * u : 8 * u + 8, :] for q in range(NX)])
                for c in range(4):
                    where = pl.ds(64 * (2 * c + u) + place(h, b), 8, stride=8)
                    upd_v[where, :] = gv[where, :] + tiles[c]

    finish()


def per_device(guesses, forcing, step_weight, land_mask, fine_matrix, coupling, coarse_matrix):
    vmem = pl.BlockSpec(memory_space=pltpu.VMEM)
    hbm = pl.BlockSpec(memory_space=pltpu.HBM)

    def in_hbm(value):
        return pltpu.with_memory_space_constraint(value, pltpu.HBM)

    flat = jax.ShapeDtypeStruct((DOF * 8, LANES), F32)
    dma = pltpu.SemaphoreType.DMA
    updated, residual = pl.pallas_call(
        kernel,
        out_shape=(flat, flat),
        in_specs=[hbm, hbm, pl.BlockSpec(memory_space=pltpu.SMEM), hbm, hbm, hbm, hbm],
        out_specs=(vmem, vmem),
        scratch_shapes=[
            pltpu.VMEM((512, LANES), F32),
            pltpu.VMEM((520, LANES), F32),
            pltpu.VMEM((512, LANES), F32),
            pltpu.VMEM((520, LANES), F32),
            pltpu.VMEM((8, LANES), jnp.int32),
            pltpu.VMEM((NX, 256, LANES), F32),
            pltpu.VMEM((NX, 264, LANES), F32),
            pltpu.VMEM((NX, 256, LANES), F32),
            pltpu.VMEM((NX, 264, LANES), F32),
            pltpu.VMEM((NX, 2, 64, LANES), F32),
            pltpu.VMEM((16, 8, LANES), F32),
            pltpu.VMEM((NX, 2, 64, LANES), F32),
            pltpu.VMEM((320, 256), BF16),
            pltpu.VMEM((512, 256), F32),
            pltpu.VMEM((512, DOF), F32),
            pltpu.VMEM((576, 256), BF16),
            pltpu.VMEM((8, 128, 256), BF16),
            pltpu.VMEM((8, 192, 256), F32),
            pltpu.VMEM((16, 64, LANES), F32),
            pltpu.VMEM((NX, 2, 64, LANES), F32),
            pltpu.VMEM((NT, 16, LANES), F32),
            pltpu.VMEM((NT, 16, LANES), F32),
            pltpu.VMEM((NZ, 64, LANES), F32),
            pltpu.VMEM((NZ - 1, 64, LANES), F32),
            pltpu.VMEM((NT, 16, LANES), F32),
            pltpu.VMEM((NX, 2, 64, LANES), F32),
            pltpu.VMEM((NT, 16, LANES), F32),
            pltpu.VMEM((DOF, DOF), F32),
            pltpu.VMEM((4 * DOF, DOF), F32),
            pltpu.VMEM((DOF, DOF), F32),
            dma((6,)), dma((2,)), dma((2,)),
            dma((NX,)), dma((NX,)), dma((NX,)), dma((NX,)), dma((NX,)), dma((NX,)),
            dma, dma, dma((NX,)), dma((NX,)), dma, dma, pltpu.SemaphoreType.REGULAR,
        ],
        compiler_params=pltpu.CompilerParams(
            collective_id=0, has_side_effects=True, vmem_limit_bytes=24 * 1024 * 1024
        ),
    )(
        in_hbm(guesses.reshape(DOF * 8, LANES)), in_hbm(forcing.reshape(DOF * 8, LANES)), step_weight, in_hbm(land_mask),
        in_hbm(fine_matrix), in_hbm(coupling.reshape(4 * DOF, DOF)), in_hbm(coarse_matrix),
    )
    return updated.reshape(guesses.shape), residual.reshape(guesses.shape)


def solution(mesh):
    tiles = P("tm", None, "gx", "gy")
    return jax.shard_map(
        per_device,
        mesh=mesh,
        in_specs=(tiles, tiles, P(), P("gx", "gy"), P(), P(), P()),
        out_specs=(tiles, tiles),
        check_vma=False,
    )
```
